256 devices in a mesh: row: 16 (over z, core), col: 16 (over y, x).
Axes of the slice: x: 4, y: 4, z: 8, core: 2. Of those that a mesh axis runs over, the one named last changes fastest.
Arguments:
- tile_values: bfloat16 [16, 16, 128, 128, 128], P('row', 'col')
- tile_rows: int32 [16, 16, 128], P('row', 'col'), may hold values from 0 to 3
- tile_cols: int32 [16, 16, 128], P('row', 'col'), may hold values from 0 to 31
- tile_counts: int32 [16, 16, 128], P('row', 'col'), may hold values from 1 to 16384
- col_factors: bfloat16 [512, 128, 128], P('col', 'row')
- prev_factors: bfloat16 [8192, 128], P('row'), may hold values from -3 to 3
Outputs:
- factors_by_rank: float32 [128, 8192], P('col', 'row')
The draws below stay inside these ranges and needn't reach their ends.
Inputs may be any that keep to these rules, and one draw needn't show every extreme that they name: `tile_rows`: row block of the tile among the 4 of the device's row group. `tile_cols`: column block of the tile among the 32 of the device's column group.
All inputs are finite; a program needn't handle non-finite values.
Results may differ from the reference program's by a relative error of at most 0.0025.
The reference program's roundings to bfloat16 on the way count: a program that leaves them out, or rounds other values in their place, can miss the bound.
Values may be sent and summed in bfloat16 or wider, within the bound.
No kernel may reach another device: no remote copies, remote signals or barrier semaphores. Data moves between devices by JAX's collectives and lax.ppermute only.
A program may use at most 64 MiB of HBM per device.

```python
import math
import jax
import jax.numpy as jnp
from jax import lax

RANK = 128
TILE = 128
RB_DEV = 4
CB_DEV = 32
NT = 128
ITERS = 3
ROW_GROUPS = 16
COL_GROUPS = 16
NCB = 512
NROWS = 8192


def draw_tile_values(key, part):
    key = jax.random.fold_in(key, 11)
    shape = (ROW_GROUPS, COL_GROUPS, NT, TILE, TILE)
    base = jax.random.normal(key, shape, jnp.float32)
    groups = shape[0]
    rising = 1.0 + 2.0 * jnp.arange(groups, dtype=jnp.float32) / max(groups - 1, 1)
    return (base * rising[:, None, None, None, None]).astype(jnp.bfloat16)


def draw_col_factors(key, part):
    key = jax.random.fold_in(key, 12)
    scale_key, value_key = jax.random.split(key)
    shape = (NCB, TILE, RANK)
    component_scale = jnp.exp(jax.random.uniform(scale_key, (RANK,), jnp.float32, math.log(0.1), 0.0))
    base = jax.random.normal(value_key, shape, jnp.float32)
    spread = (NCB * TILE) ** (-0.5)
    return (base * component_scale[None, None, :] * spread).astype(jnp.bfloat16)


def plant(entries, rng, low, top_value):
    longest = entries.shape.index(max(entries.shape))
    spots = []
    for shift in (0, 1):
        where = [jax.random.randint(jax.random.fold_in(rng, axis), (), 0, length) for axis, length in enumerate(entries.shape)]
        where[longest] = (where[longest] + shift) % entries.shape[longest]
        spots.append(tuple(where))
    return entries.at[spots[0]].set(low).at[spots[1]].set(top_value)


def shard_levels(own_key, extent, pieces, low, top_value):
    def one(axis_at, blocks):
        draws = jax.random.uniform(jax.random.fold_in(jax.random.fold_in(own_key, 6), axis_at), (blocks,), jnp.float32, low / len(pieces), top_value / len(pieces))
        return jnp.repeat(jnp.exp(draws), extent[axis_at] // blocks).reshape((-1,) + (1,) * (len(extent) - axis_at - 1))

    level = one(*pieces[0])
    for cut in pieces[1:]:
        level = level * one(*cut)
    return level


def centred(rng, shape, scale, bound, cuts=(), kind=jnp.bfloat16):
    loudness = shard_levels(rng, shape, cuts, -0.22, 0.18) if cuts else 1.0
    entries = jax.random.normal(rng, shape, jnp.float32) * scale * loudness
    return jnp.minimum(jnp.maximum(entries, -bound), bound).astype(kind)


def setup_inputs(seed: int = 0) -> dict:
    splits = jax.random.split(jax.random.key(seed), 7)
    return {
        "tile_values": draw_tile_values(jax.random.fold_in(splits[6], 71), 0),
        "tile_rows": plant(jax.random.randint(splits[1], (ROW_GROUPS, COL_GROUPS, NT), 0, RB_DEV), jax.random.fold_in(splits[1], 1), 0, RB_DEV - 1).astype(jnp.int32),
        "tile_cols": plant(jax.random.randint(splits[2], (ROW_GROUPS, COL_GROUPS, NT), 0, CB_DEV), jax.random.fold_in(splits[2], 1), 0, CB_DEV - 1).astype(jnp.int32),
        "tile_counts": plant(jax.random.randint(splits[3], (ROW_GROUPS, COL_GROUPS, NT), 1, TILE * TILE + 1), jax.random.fold_in(splits[3], 1), 1, TILE * TILE).astype(jnp.int32),
        "col_factors": draw_col_factors(jax.random.fold_in(splits[6], 71), 0),
        "prev_factors": centred(splits[5], (NROWS, RANK), 0.5, 3.0, ((0, 16),)),
    }


ridge_weight = 0.1
epsilon = 1e-12


def reference(tile_values, tile_rows, tile_cols, tile_counts, col_factors, prev_factors):
    rank_width = col_factors.shape[2]
    flattened = col_factors.reshape(-1, rank_width)
    gramian = jnp.dot(flattened.T, flattened, preferred_element_type=jnp.float32)
    grouped = col_factors.reshape(COL_GROUPS, CB_DEV, TILE, rank_width)
    highest = lax.Precision.HIGHEST

    def slab_data(slab_half, linear):
        blocked = slab_half.reshape(ROW_GROUPS, RB_DEV, TILE, rank_width)

        def one_slab(row_group):
            zblocks = blocked[row_group]

            def one_device(carry, col_group):
                values = tile_values[row_group, col_group].astype(jnp.float32)
                tile_row = tile_rows[row_group, col_group]
                tile_col = tile_cols[row_group, col_group]
                density = tile_counts[row_group, col_group].astype(jnp.float32) / (TILE * TILE)
                ztiles = jnp.take(zblocks, tile_row, axis=0).astype(jnp.float32)
                vtiles = jnp.take(grouped[col_group], tile_col, axis=0).astype(jnp.float32)
                scores = jnp.einsum('tik,tjk->tij', ztiles, vtiles, precision=highest)
                weights = density[:, None, None] * values * values * scores
                if linear:
                    weights = density[:, None, None] * values - weights
                rounded = lax.optimization_barrier(weights.astype(jnp.bfloat16)).astype(jnp.float32)
                row_terms = jnp.einsum('tij,tjk->tik', rounded, vtiles, precision=highest)
                summed = jax.ops.segment_sum(row_terms, tile_row, RB_DEV)
                return carry + summed, None

            start = jnp.zeros((RB_DEV, TILE, rank_width), jnp.float32)
            total_sum, unused = lax.scan(one_device, start, jnp.arange(COL_GROUPS))
            return total_sum

        return lax.map(one_slab, jnp.arange(ROW_GROUPS)).reshape(-1, rank_width)

    def operate(direction):
        data = slab_data(direction.astype(jnp.bfloat16), False)
        return data + jnp.dot(direction, gramian, precision=highest) + ridge_weight * direction

    solution = prev_factors.astype(jnp.float32)
    residual = slab_data(prev_factors, True) - jnp.dot(solution, gramian, precision=highest) - ridge_weight * solution
    direction = residual
    norm_now = jnp.sum(residual * residual)
    for iteration in range(ITERS):
        image = operate(direction)
        step_size = norm_now / (jnp.sum(direction * image) + epsilon)
        solution = solution + step_size * direction
        residual = residual - step_size * image
        if iteration + 1 < ITERS:
            norm_next = jnp.sum(residual * residual)
            direction = residual + (norm_next / (norm_now + epsilon)) * direction
            norm_now = norm_next
    return solution.T
```

```python
import functools

import jax
import jax.numpy as jnp
from jax import lax
from jax.experimental import pallas as pl
from jax.experimental.pallas import tpu as pltpu
from jax.sharding import PartitionSpec as P

ITERS = 3
RIDGE = 0.1
EPS = 1e-12
UNROLL = 8
F32 = jnp.float32
BF16 = jnp.bfloat16
NT_DIMS = (((1,), (1,)), ((), ()))
VMEM = pltpu.VMEM
SMEM = pltpu.SMEM


def spec(space):
    return pl.BlockSpec(memory_space=space)


def call(kernel, out_shape, in_spaces, scratch=()):
    single = not isinstance(out_shape, (list, tuple))
    return pl.pallas_call(
        kernel,
        out_shape=out_shape,
        in_specs=[spec(s) for s in in_spaces],
        out_specs=spec(VMEM) if single else [spec(VMEM) for _ in out_shape],
        scratch_shapes=list(scratch),
        compiler_params=pltpu.CompilerParams(vmem_limit_bytes=40 * 1024 * 1024),
    )


def data_product(flag, rows, cols, dens, tiles, factors, zb, acc):
    count = tiles.shape[0]

    def group(g, carry):
        ids = [g * UNROLL + u for u in range(UNROLL)]
        weights = []
        for t in ids:
            scores = lax.dot_general(
                zb[rows[t]], factors[cols[t]], NT_DIMS, preferred_element_type=F32
            )
            values = tiles[t].astype(F32)
            scaled = dens[t] * values
            w = scaled * values * scores
            if flag:
                w = scaled - w
            weights.append(w.astype(BF16))
        for t, w in zip(ids, weights):
            acc[rows[t]] += jnp.dot(w, factors[cols[t]], preferred_element_type=F32)
        return carry

    lax.fori_loop(0, count // UNROLL, group, 0)


def gram_product(p, gram):
    return jnp.dot(p, gram, precision=lax.Precision.HIGHEST, preferred_element_type=F32)


def first_kernel(rows, cols, dens, tiles, factors, gram, prev, out):
    blocks, size = out.shape[0], out.shape[1]
    p = prev[...].astype(F32)
    out[...] = -gram_product(p.reshape(blocks * size, -1), gram[...]).reshape(out.shape)
    data_product(True, rows, cols, dens, tiles, factors, prev, out)


def residual_kernel(me, parts, prev, out):
    n, height = parts.shape[0], parts.shape[1]
    total = jnp.sum(parts[...], axis=0)
    mine = prev[pl.ds(pl.multiple_of(me[0] * height, height), height), :].astype(F32)
    shard = total - RIDGE * mine
    out[...] = jnp.broadcast_to(shard[None], out.shape)


def lanes(*scalars):
    lane = lax.broadcasted_iota(jnp.int32, (8, 128), 1)
    row = jnp.zeros((8, 128), F32)
    for i, s in enumerate(scalars):
        row = jnp.where(lane == i, s, row)
    return row


def total11(x):
    return jnp.sum(jnp.sum(x, axis=0, keepdims=True), axis=1, keepdims=True)


def max11(x):
    return jnp.max(jnp.max(x, axis=0, keepdims=True), axis=1, keepdims=True)


def lane_of(x, i):
    return x[..., i : i + 1]


def start_kernel(rows, cols, dens, tiles, factors, gram, slab_parts, out, direction, zb):
    blocks, size, width = out.shape
    r = slab_parts[...].reshape(blocks * size, width)
    direction[...] = r
    zb[...] = r.astype(BF16).reshape(zb.shape)
    out[...] = gram_product(r, gram[...]).reshape(out.shape)
    data_product(False, rows, cols, dens, tiles, factors, zb, out)


def image_kernel(me, parts, direction, residual, image, sums):
    height = parts.shape[1]
    at = pl.ds(pl.multiple_of(me[0] * height, height), height)
    p = direction[at, :]
    r = residual[at, :]
    im = jnp.sum(parts[...], axis=0) + RIDGE * p
    image[...] = im
    top = max11(jnp.abs(im))
    unit = im * jnp.where(top > 0, 1.0 / top, 0.0)
    row = lanes(total11(p * im), total11(r * im), total11(r * r), total11(unit * unit), top)
    sums[...] = jnp.broadcast_to(row[None, :1], sums.shape)


def merge(rows):
    top = jnp.max(lane_of(rows, 4), axis=0, keepdims=True)
    ratio = lane_of(rows, 4) * jnp.where(top > 0, 1.0 / top, 0.0)
    square = jnp.sum(lane_of(rows, 3) * ratio * ratio, axis=0, keepdims=True)
    sums = jnp.sum(rows, axis=0, keepdims=True)
    return lane_of(sums, 0), lane_of(sums, 1), lane_of(sums, 2), square, top


def payload_kernel(sums, image, out):
    height = image.shape[0]
    n = out.shape[0]
    row = lanes(*merge(sums[:, 0, :]))
    block = jnp.concatenate([image[...], row], axis=0)
    out[...] = jnp.broadcast_to(block[None], out.shape)


def step_kernel(
    rows, cols, dens, tiles, factors, gram, gathered, sol, res, direction,
    out, sol_out, res_out, direction_out, zb,
):
    blocks, size, width = out.shape
    height = gathered.shape[1] - 8
    image = gathered[:, :height, :].reshape(blocks * size, width)
    curvature, cross, norm, square, top = merge(gathered[:, height, :])
    step = norm / (curvature + EPS)
    p, r = direction[...], res[...]
    scaled = step * top
    following = jnp.maximum(norm - 2.0 * (step * cross) + scaled * scaled * square, 0.0)
    sol_out[...] = sol[...] + step * p
    r = r - step * image
    res_out[...] = r
    p = r + following / (norm + EPS) * p
    direction_out[...] = p
    zb[...] = p.astype(BF16).reshape(zb.shape)
    out[...] = gram_product(p, gram[...]).reshape(out.shape)
    data_product(False, rows, cols, dens, tiles, factors, zb, out)


def last_sums_kernel(parts, direction, residual, out):
    groups = 16.0
    p, r = direction[...], residual[...]
    a = total11(p * parts[...].reshape(p.shape) + p * p * (RIDGE / groups))
    b = total11(r * r * (1.0 / groups))
    out[...] = jnp.broadcast_to(lanes(a, b)[:1], out.shape)


def finish_kernel(sums, sol, direction, out):
    rows = sums[...]
    total = jnp.sum(rows, axis=0, keepdims=True)
    step = lane_of(total, 1) / (lane_of(total, 0) + EPS)
    out[...] = sol[...] + step * direction[...]


def local(tile_values, tile_rows, tile_cols, tile_counts, col_factors, prev_factors):
    tiles = tile_values[0, 0]
    rows, cols = tile_rows[0, 0], tile_cols[0, 0]
    count, size = tiles.shape[0], tiles.shape[1]
    dens = tile_counts[0, 0].astype(F32) / (size * size)
    width = col_factors.shape[2]
    blocks = prev_factors.shape[0] // size
    height_all = blocks * size
    ncol, nrow = lax.axis_size("col"), lax.axis_size("row")
    height = height_all // ncol
    me = lax.axis_index("col").astype(jnp.int32).reshape(1)

    sent = jnp.broadcast_to(col_factors[None], (nrow,) + col_factors.shape)
    got = lax.all_to_all(sent, "row", 0, 0)
    factors = got.transpose(1, 0, 2, 3).reshape(col_factors.shape[0], size, width)
    flat = factors.reshape(-1, width)
    gram = lax.dot_general(flat, flat, (((0,), (0,)), ((), ())), preferred_element_type=F32)

    def exchange(x):
        return lax.all_to_all(x, "col", 0, 0)

    slab = jax.ShapeDtypeStruct((height_all, width), F32)
    part = jax.ShapeDtypeStruct((blocks, size, width), F32)
    shard = jax.ShapeDtypeStruct((height, width), F32)
    zb = VMEM((blocks, size, width), BF16)
    common = (rows, cols, dens, tiles, factors, gram)
    spaces = [SMEM, SMEM, SMEM, VMEM, VMEM, VMEM]

    partial = call(first_kernel, part, spaces + [VMEM])(
        *common, prev_factors.reshape(blocks, size, width)
    )
    parts = exchange(partial.reshape(ncol, height, width))
    wide = jax.ShapeDtypeStruct((ncol, height, width), F32)
    sent = call(residual_kernel, wide, [SMEM, VMEM, VMEM])(me, parts, prev_factors)
    gathered = exchange(sent)
    partial, direction = call(start_kernel, [part, slab], spaces + [VMEM], [zb])(
        *common, gathered
    )
    residual = direction
    sol = prev_factors.astype(F32)
    for _ in range(ITERS - 1):
        parts = exchange(partial.reshape(ncol, height, width))
        image, sums = call(
            image_kernel,
            [shard, jax.ShapeDtypeStruct((nrow, 1, width), F32)],
            [SMEM, VMEM, VMEM, VMEM],
        )(me, parts, direction, residual)
        sums = lax.all_to_all(sums, "row", 0, 0)
        sent = call(
            payload_kernel, jax.ShapeDtypeStruct((ncol, height + 8, width), F32), [VMEM, VMEM]
        )(sums, image)
        gathered = exchange(sent)
        partial, sol, residual, direction = call(
            step_kernel, [part, slab, slab, slab], spaces + [VMEM] * 4, [zb]
        )(*common, gathered, sol, residual, direction)
    sums = call(
        last_sums_kernel, jax.ShapeDtypeStruct((nrow * ncol, width), F32), [VMEM] * 3
    )(partial, direction, residual)
    sums = lax.all_to_all(sums, ("row", "col"), 0, 0, tiled=True)
    components = width // ncol
    at = lax.axis_index("col") * components
    sol_part = lax.dynamic_slice_in_dim(sol, at, components, 1).T
    direction_part = lax.dynamic_slice_in_dim(direction, at, components, 1).T
    return call(
        finish_kernel, jax.ShapeDtypeStruct((components, height_all), F32), [VMEM] * 3
    )(sums, sol_part, direction_part)


def solution(mesh):
    return jax.shard_map(
        local,
        mesh=mesh,
        in_specs=(
            P("row", "col", None, None, None),
            P("row", "col", None),
            P("row", "col", None),
            P("row", "col", None),
            P("col", "row", None),
            P("row", None),
        ),
        out_specs=P("col", "row"),
        check_vma=False,
    )
```

```python
import functools

import jax
import jax.numpy as jnp
from jax import lax
from jax.experimental import pallas as pl
from jax.experimental.pallas import tpu as pltpu
from jax.sharding import PartitionSpec as P

RIDGE = 0.1
EPS = 1e-12
F32 = jnp.float32
BF16 = jnp.bfloat16
NT_DIMS = (((1,), (1,)), ((), ()))
VMEM = pltpu.VMEM
SMEM = pltpu.SMEM


def spec(space):
    return pl.BlockSpec(memory_space=space)


def call(kernel, out_shape, in_spaces, scratch=()):
    single = not isinstance(out_shape, (list, tuple))
    return pl.pallas_call(
        kernel,
        out_shape=out_shape,
        in_specs=[spec(s) for s in in_spaces],
        out_specs=spec(VMEM) if single else [spec(VMEM) for _ in out_shape],
        scratch_shapes=list(scratch),
        compiler_params=pltpu.CompilerParams(vmem_limit_bytes=16 * 1024 * 1024),
    )


def plan(rows, cols, dens, blocks):
    t = jnp.arange(rows.shape[0])
    r = jnp.arange(blocks)
    s = jnp.arange(rows.shape[0] + blocks)
    earlier = (rows[:, None] == rows[None, :]) & (t[None, :] < t[:, None])
    rank = jnp.sum(earlier, axis=1)
    held = jnp.sum(rows[None, :] == r[:, None], axis=1)
    held = (held + 1) // 2 * 2
    start = jnp.sum(jnp.where(r[None, :] < r[:, None], held[None, :], 0), axis=1)
    slot = rank + jnp.sum(jnp.where(rows[:, None] == r[None, :], start[None, :], 0), axis=1)
    hit = slot[None, :] == s[:, None]
    ids = jnp.sum(jnp.where(hit, t[None, :], 0), axis=1)
    slot_cols = jnp.sum(jnp.where(hit, cols[None, :], 0), axis=1)
    slot_dens = jnp.sum(jnp.where(hit, dens[None, :], 0.0), axis=1)
    pair_rows = jnp.sum(s[::2][:, None] >= start[None, 1:], axis=1)
    return ids.astype(jnp.int32), slot_cols.astype(jnp.int32), slot_dens, pair_rows.astype(jnp.int32)


def data_product(flag, ids, cols, dens, rows, tiles, factors, zb, acc):
    pairs = rows.shape[0]
    unroll = max(u for u in range(1, 25) if pairs % u == 0)

    def group(g, carry):
        held = []
        for u in range(unroll):
            pair = g * unroll + u
            slots = (2 * pair, 2 * pair + 1)
            both = jnp.concatenate([factors[cols[s]] for s in slots], axis=0)
            scores = lax.dot_general(zb[rows[pair]], both, NT_DIMS, preferred_element_type=F32)
            weights = []
            for s, score in zip(slots, jnp.split(scores, 2, axis=1)):
                values = tiles[ids[s]].astype(F32)
                scaled = dens[s] * values
                w = scaled * values * score
                if flag:
                    w = scaled - w
                weights.append(w.astype(BF16))
            held.append((rows[pair], jnp.concatenate(weights, axis=1), both))
        for row, w, both in held:
            acc[row] += jnp.dot(w, both, preferred_element_type=F32)
        return carry

    lax.fori_loop(0, pairs // unroll, group, 0)


def gram_product(p, gram):
    return jnp.dot(p, gram, precision=lax.Precision.HIGHEST, preferred_element_type=F32)


def total11(x):
    return jnp.sum(jnp.sum(x, axis=0, keepdims=True), axis=1, keepdims=True)


def dot11(x, y):
    return total11(x * y)


def lanes(scalars):
    lane = lax.broadcasted_iota(jnp.int32, (1, 128), 1)
    row = jnp.zeros((1, 128), F32)
    for i, s in enumerate(scalars):
        row = jnp.where(lane == i, s, row)
    return row


def ratio(top, below, otherwise):
    good = (top > 0.0) & (below > 0.0)
    value = top / jnp.where(good, below, 1.0)
    return jnp.where(good, jnp.clip(value, 1e-30, 1e30), otherwise)


def apply_first(ids, cols, dens, rows, tiles, factors, gram, prev, out):
    blocks, size, width = out.shape
    p = prev[...].astype(F32).reshape(blocks * size, width)
    out[...] = -gram_product(p, gram[...]).reshape(out.shape)
    data_product(True, ids, cols, dens, rows, tiles, factors, prev, out)


def apply_operator(ids, cols, dens, rows, tiles, factors, gram, p, zb, out):
    zb[...] = p.astype(BF16).reshape(zb.shape)
    out[...] = gram_product(p, gram[...]).reshape(out.shape)
    data_product(False, ids, cols, dens, rows, tiles, factors, zb, out)


def shard_of(me, parts, slab, sign):
    height = parts.shape[1]
    mine = slab[pl.ds(pl.multiple_of(me[0] * height, height), height), :].astype(F32)
    return jnp.sum(parts[...], axis=0) + sign * RIDGE * mine, mine


def shard_kernel(sign, me, parts, slab, out):
    shard, _ = shard_of(me, parts, slab, sign)
    out[...] = jnp.broadcast_to(shard[None], out.shape)


def image_kernel(me, parts, slab, image, sums):
    shard, mine = shard_of(me, parts, slab, 1.0)
    image[...] = shard
    top = jnp.max(jnp.max(jnp.abs(shard), axis=0, keepdims=True), axis=1, keepdims=True)
    unit = shard * jnp.where(top > 0.0, 1.0 / top, 0.0)
    row = lanes([dot11(mine, shard), dot11(mine, mine), dot11(unit, unit), top])
    sums[...] = jnp.broadcast_to(row[None], sums.shape)


def merge(rows):
    top = jnp.max(rows[:, 3:4], axis=0, keepdims=True)
    scale = rows[:, 3:4] * jnp.where(top > 0.0, 1.0 / top, 0.0)
    square = jnp.sum(rows[:, 2:3] * scale * scale, axis=0, keepdims=True)
    total = jnp.sum(rows, axis=0, keepdims=True)
    return total[:, 0:1], total[:, 1:2], square, top


def payload_kernel(sums, image, out):
    row = jnp.broadcast_to(lanes(merge(sums[:, 0, :])), (8, sums.shape[-1]))
    block = jnp.concatenate([image[...], row], axis=0)
    out[...] = jnp.broadcast_to(block[None], out.shape)


def product0_kernel(ids, cols, dens, rows, tiles, factors, gram, gathered, out, q0, zb):
    q = gathered[...].reshape(q0.shape)
    q0[...] = q
    apply_operator(ids, cols, dens, rows, tiles, factors, gram, q, zb, out)


def product1_kernel(
    ids, cols, dens, rows, tiles, factors, gram, gathered, q0, out, q1, res1, image0, scalars, zb,
):
    height = gathered.shape[1] - 8
    q, v = q0[...], gathered[:, :height, :].reshape(q0.shape)
    image0[...] = v
    curvature, norm, square, top = merge(gathered[:, height, :])
    step = norm / (curvature + EPS)
    scaled = step * top
    following = jnp.maximum(norm - 2.0 * (step * curvature) + scaled * scaled * square, 0.0)
    turn = following / (norm + EPS)
    scalars[...] = jnp.broadcast_to(lanes([step, turn]), scalars.shape)
    r = q - step * v
    res1[...] = r
    q = r + turn * q
    q1[...] = q
    apply_operator(ids, cols, dens, rows, tiles, factors, gram, q, zb, out)


def product2_kernel(
    shares, ids, cols, dens, rows, tiles, factors, gram, gathered, image0, q0, q1, res1,
    sums, q2, zb, out,
):
    q, p, r = q0[...], q1[...], res1[...]
    v0, v1 = image0[...], gathered[...].reshape(q.shape)
    c00, c01, c10, c11 = dot11(q, v0), dot11(q, v1), dot11(p, v0), dot11(p, v1)
    n11 = dot11(r, r)
    a1 = ratio(n11, c11, 1.0)
    r2 = r - a1 * v1
    n12, n22 = dot11(r, r2), dot11(r2, r2)
    b1 = ratio(n22, n11, 0.0)
    q_two = r2 + b1 * p
    q2[...] = q_two
    apply_operator(ids, cols, dens, rows, tiles, factors, gram, q_two, zb, out)
    share = 1.0 / shares
    v2 = out[...].reshape(q.shape) + (RIDGE * share) * q_two
    shared = [n11, n12, n22, c00, c01, c10, c11, a1, b1]
    row = lanes([s * share for s in shared] + [dot11(q, v2), dot11(p, v2), dot11(q_two, v2)])
    sums[...] = jnp.broadcast_to(row[None], sums.shape)


def finish_kernel(shares, me, sums, scalars, x0, q0, q1, q2, out):
    rows = jnp.sum(sums[...].reshape(-1, shares, sums.shape[-1]), axis=1)
    n11, n12, n22, c00, c01, c10, c11, a1, b1, c02, c12, c22 = (rows[:, i : i + 1] for i in range(12))
    step0, turn0 = scalars[:1, 0:1], scalars[:1, 1:2]

    def over_rows(x):
        return jnp.sum(x, axis=0, keepdims=True)

    norm1 = over_rows(n11)
    step1 = norm1 / (over_rows(c11) + EPS)
    h = step1 / a1
    rest = 1.0 - h
    norm2 = over_rows(rest * rest * n11 + 2.0 * h * rest * n12 + h * h * n22)
    turn1 = norm2 / (norm1 + EPS)
    g0 = -rest * turn0
    g1 = rest + turn1 - h * b1
    curvature = over_rows(
        g0 * g0 * c00 + g1 * g1 * c11 + h * h * c22
        + g0 * g1 * (c01 + c10) + 2.0 * (g0 * h * c02 + g1 * h * c12)
    )
    step2 = norm2 / (curvature + EPS)
    mine = lax.broadcasted_iota(jnp.int32, a1.shape, 0) == me[0]

    def own(x):
        return over_rows(jnp.where(mine, x, 0.0))

    k0, k1, k2 = own(step0 + step2 * g0), own(step1 + step2 * g1), own(step2 * h)
    out[...] = x0[...].astype(F32) + k0 * q0[...] + k1 * q1[...] + k2 * q2[...]


def gather_factors(col_factors):
    nrow = lax.axis_size("row")
    blocks, height, width = col_factors.shape
    groups = [list(range(core, nrow, 2)) for core in range(2)]
    sent = jnp.broadcast_to(col_factors[None], (nrow // 2,) + col_factors.shape)
    mine = lax.all_to_all(sent, "row", 0, 0, axis_index_groups=groups)
    other = lax.ppermute(mine, "row", [(i, i ^ 1) for i in range(nrow)])
    first = lax.axis_index("row") % 2 == 0
    both = jnp.stack([jnp.where(first, mine, other), jnp.where(first, other, mine)], axis=1)
    return both.transpose(2, 0, 1, 3, 4).reshape(blocks, nrow * height, width)


def local(tile_values, tile_rows, tile_cols, tile_counts, col_factors, prev_factors):
    tiles = tile_values[0, 0]
    size = tiles.shape[1]
    width = col_factors.shape[2]
    height_all = prev_factors.shape[0]
    blocks = height_all // size
    ncol, nrow = lax.axis_size("col"), lax.axis_size("row")
    height = height_all // ncol
    at_col = lax.axis_index("col").astype(jnp.int32).reshape(1)
    at_row = lax.axis_index("row").astype(jnp.int32).reshape(1)

    dens = tile_counts[0, 0].astype(F32) / (size * size)
    order = plan(tile_rows[0, 0], tile_cols[0, 0], dens, blocks)
    factors = gather_factors(col_factors)
    flat = factors.reshape(-1, width)
    gram = lax.dot_general(flat, flat, (((0,), (0,)), ((), ())), preferred_element_type=F32)

    def exchange(x):
        return lax.all_to_all(x, "col", 0, 0)

    slab = jax.ShapeDtypeStruct((height_all, width), F32)
    part = jax.ShapeDtypeStruct((blocks, size, width), F32)
    wide = jax.ShapeDtypeStruct((ncol, height, width), F32)
    zb = VMEM((blocks, size, width), BF16)
    common = (*order, tiles, factors, gram)
    spaces = [SMEM] * 4 + [VMEM] * 3

    def summed(sign, partial, p):
        parts = exchange(partial.reshape(ncol, height, width))
        shard = call(functools.partial(shard_kernel, sign), wide, [SMEM, VMEM, VMEM])
        return exchange(shard(at_col, parts, p))

    partial = call(apply_first, part, spaces + [VMEM])(
        *common, prev_factors.reshape(blocks, size, width)
    )
    res0 = summed(-1.0, partial, prev_factors)
    partial, q0 = call(product0_kernel, [part, slab], spaces + [VMEM], [zb])(*common, res0)
    parts = exchange(partial.reshape(ncol, height, width))
    image, sums = call(
        image_kernel,
        [jax.ShapeDtypeStruct((height, width), F32), jax.ShapeDtypeStruct((nrow, 1, width), F32)],
        [SMEM, VMEM, VMEM],
    )(at_col, parts, q0)
    sums = lax.all_to_all(sums, "row", 0, 0)
    payload = jax.ShapeDtypeStruct((ncol, height + 8, width), F32)
    gathered = exchange(call(payload_kernel, payload, [VMEM, VMEM])(sums, image))
    small = jax.ShapeDtypeStruct((8, width), F32)
    partial, q1, res1, image0, scalars = call(
        product1_kernel, [part, slab, slab, slab, small], spaces + [VMEM] * 2, [zb]
    )(*common, gathered, q0)
    gathered = summed(1.0, partial, q1)
    sums, q2 = call(
        functools.partial(product2_kernel, ncol),
        [jax.ShapeDtypeStruct((nrow * ncol, 1, width), F32), slab],
        spaces + [VMEM] * 5,
        [zb, VMEM((blocks, size, width), F32)],
    )(*common, gathered, image0, q0, q1, res1)
    sums = lax.all_to_all(sums, ("row", "col"), 0, 0, tiled=True)
    components = width // ncol

    def piece(x):
        return lax.dynamic_slice_in_dim(x, at_col[0] * components, components, 1).T

    return call(
        functools.partial(finish_kernel, ncol),
        jax.ShapeDtypeStruct((components, height_all), F32),
        [SMEM] + [VMEM] * 6,
    )(at_row, sums, scalars, piece(prev_factors.astype(F32)), piece(q0), piece(q1), piece(q2))


def solution(mesh):
    return jax.shard_map(
        local,
        mesh=mesh,
        in_specs=(
            P("row", "col", None, None, None),
            P("row", "col", None),
            P("row", "col", None),
            P("row", "col", None),
            P("col", "row", None),
            P("row", None),
        ),
        out_specs=P("col", "row"),
        check_vma=False,
    )
```

```python
import functools

import jax
import jax.numpy as jnp
from jax import lax
from jax.experimental import pallas as pl
from jax.experimental.pallas import tpu as pltpu
from jax.sharding import PartitionSpec as P

RIDGE = 0.1
EPS = 1e-12
F32 = jnp.float32
BF16 = jnp.bfloat16
NT_DIMS = (((1,), (1,)), ((), ()))
VMEM = pltpu.VMEM
SMEM = pltpu.SMEM


def spec(space):
    return pl.BlockSpec(memory_space=space)


def call(kernel, out_shape, in_spaces, scratch=()):
    single = not isinstance(out_shape, (list, tuple))
    return pl.pallas_call(
        kernel,
        out_shape=out_shape,
        in_specs=[spec(s) for s in in_spaces],
        out_specs=spec(VMEM) if single else [spec(VMEM) for _ in out_shape],
        scratch_shapes=list(scratch),
        compiler_params=pltpu.CompilerParams(vmem_limit_bytes=16 * 1024 * 1024),
    )


def plan(rows, cols, dens, blocks):
    t = jnp.arange(rows.shape[0])
    r = jnp.arange(blocks)
    s = jnp.arange(rows.shape[0] + blocks)
    earlier = (rows[:, None] == rows[None, :]) & (t[None, :] < t[:, None])
    rank = jnp.sum(earlier, axis=1)
    held = jnp.sum(rows[None, :] == r[:, None], axis=1)
    held = (held + 1) // 2 * 2
    start = jnp.sum(jnp.where(r[None, :] < r[:, None], held[None, :], 0), axis=1)
    slot = rank + jnp.sum(jnp.where(rows[:, None] == r[None, :], start[None, :], 0), axis=1)
    hit = slot[None, :] == s[:, None]
    ids = jnp.sum(jnp.where(hit, t[None, :], 0), axis=1)
    slot_cols = jnp.sum(jnp.where(hit, cols[None, :], 0), axis=1)
    slot_dens = jnp.sum(jnp.where(hit, dens[None, :], 0.0), axis=1)
    pair_rows = jnp.sum(s[::2][:, None] >= start[None, 1:], axis=1)
    return ids.astype(jnp.int32), slot_cols.astype(jnp.int32), slot_dens, pair_rows.astype(jnp.int32)


def confidence_kernel(ids, dens, tiles, out):
    def one(s, carry):
        values = tiles[ids[s]].astype(F32)
        out[s] = dens[s] * values * values
        return carry

    lax.fori_loop(0, out.shape[0], one, 0, unroll=6)


def unroll_of(pairs):
    return max(u for u in range(1, 25) if pairs % u == 0)


def pair_scores(pair, cols, rows, factors, zb):
    slots = (2 * pair, 2 * pair + 1)
    both = jnp.concatenate([factors[cols[s]] for s in slots], axis=0)
    scores = lax.dot_general(zb[rows[pair]], both, NT_DIMS, preferred_element_type=F32)
    return both, list(zip(slots, jnp.split(scores, 2, axis=1)))


def data_product(cols, rows, conf, factors, zb, acc, flagged=None):
    pairs = rows.shape[0]
    unroll = unroll_of(pairs)

    def group(g, carry):
        held = []
        for u in range(unroll):
            pair = g * unroll + u
            both, scores = pair_scores(pair, cols, rows, factors, zb)
            weights = []
            for s, score in scores:
                w = conf[s] * score
                if flagged is not None:
                    ids, dens, tiles = flagged
                    w = dens[s] * tiles[ids[s]].astype(F32) - w
                weights.append(w.astype(BF16))
            held.append((rows[pair], jnp.concatenate(weights, axis=1), both))
        for row, w, both in held:
            acc[row] += jnp.dot(w, both, preferred_element_type=F32)
        return carry

    lax.fori_loop(0, pairs // unroll, group, 0)


def data_curvature(cols, rows, conf, factors, zb):
    pairs = rows.shape[0]
    unroll = unroll_of(pairs)

    def group(g, total):
        for u in range(unroll):
            _, scores = pair_scores(g * unroll + u, cols, rows, factors, zb)
            for s, score in scores:
                total = total + jnp.sum((conf[s] * score * score).reshape(-1, 8, 128), axis=0)
        return total

    return lax.fori_loop(0, pairs // unroll, group, jnp.zeros((8, 128), F32))


def gram_product(p, gram):
    return jnp.dot(p, gram, precision=lax.Precision.HIGHEST, preferred_element_type=F32)


def total11(x):
    return jnp.sum(jnp.sum(x, axis=0, keepdims=True), axis=1, keepdims=True)


def dot11(x, y):
    return total11(x * y)


def lanes(scalars):
    lane = lax.broadcasted_iota(jnp.int32, (1, 128), 1)
    row = jnp.zeros((1, 128), F32)
    for i, s in enumerate(scalars):
        row = jnp.where(lane == i, s, row)
    return row


def apply_first(ids, dens, tiles, cols, rows, conf, factors, gram, prev, out):
    blocks, size, width = out.shape
    p = prev[...].astype(F32).reshape(blocks * size, width)
    out[...] = -gram_product(p, gram[...]).reshape(out.shape)
    data_product(cols, rows, conf, factors, prev, out, (ids, dens, tiles))


def apply_operator(cols, rows, conf, factors, gram, p, zb, out):
    zb[...] = p.astype(BF16).reshape(zb.shape)
    out[...] = gram_product(p, gram[...]).reshape(out.shape)
    data_product(cols, rows, conf, factors, zb, out)


def shard_of(me, parts, slab, sign):
    height = parts.shape[1]
    mine = slab[pl.ds(pl.multiple_of(me[0] * height, height), height), :].astype(F32)
    return jnp.sum(parts[...], axis=0) + sign * RIDGE * mine, mine


def shard_kernel(sign, me, parts, slab, out):
    shard, _ = shard_of(me, parts, slab, sign)
    out[...] = jnp.broadcast_to(shard[None], out.shape)


def image_kernel(me, parts, slab, image, sums):
    shard, mine = shard_of(me, parts, slab, 1.0)
    image[...] = shard
    top = jnp.max(jnp.max(jnp.abs(shard), axis=0, keepdims=True), axis=1, keepdims=True)
    unit = shard * jnp.where(top > 0.0, 1.0 / top, 0.0)
    row = lanes([dot11(mine, shard), dot11(mine, mine), dot11(unit, unit), top])
    sums[...] = jnp.broadcast_to(row[None], sums.shape)


def merge(rows):
    top = jnp.max(rows[:, 3:4], axis=0, keepdims=True)
    scale = rows[:, 3:4] * jnp.where(top > 0.0, 1.0 / top, 0.0)
    square = jnp.sum(rows[:, 2:3] * scale * scale, axis=0, keepdims=True)
    total = jnp.sum(rows, axis=0, keepdims=True)
    return total[:, 0:1], total[:, 1:2], square, top


def payload_kernel(sums, image, out):
    row = jnp.broadcast_to(lanes(merge(sums[:, 0, :])), (8, sums.shape[-1]))
    block = jnp.concatenate([image[...], row], axis=0)
    out[...] = jnp.broadcast_to(block[None], out.shape)


def product0_kernel(cols, rows, conf, factors, gram, gathered, out, q0, zb):
    q = gathered[...].reshape(q0.shape)
    q0[...] = q
    apply_operator(cols, rows, conf, factors, gram, q, zb, out)


def product1_kernel(
    cols, rows, conf, factors, gram, gathered, q0, out, q1, res1, image0, scalars, zb,
):
    height = gathered.shape[1] - 8
    q, v = q0[...], gathered[:, :height, :].reshape(q0.shape)
    image0[...] = v
    curvature, norm, square, top = merge(gathered[:, height, :])
    step = norm / (curvature + EPS)
    scaled = step * top
    following = jnp.maximum(norm - 2.0 * (step * curvature) + scaled * scaled * square, 0.0)
    turn = following / (norm + EPS)
    scalars[...] = jnp.broadcast_to(lanes([step, turn]), scalars.shape)
    r = q - step * v
    res1[...] = r
    q = r + turn * q
    q1[...] = q
    apply_operator(cols, rows, conf, factors, gram, q, zb, out)


def trial(scalars):
    step, turn = scalars[:1, 0:1], scalars[:1, 1:2]
    usable = (step > 1e-30) & (step < 1e30)
    return step, turn, jnp.where(usable, step, 1.0), jnp.where(usable, turn, 0.0)


def product2_kernel(
    me, cols, rows, conf, factors, gram, gathered, scalars, image0, q0, q1, res1, sums, q2, zb,
):
    _, _, a, b = trial(scalars)
    slab = q2.shape
    q_two = res1[...] - a * gathered[...].reshape(slab) + b * q1[...]
    q2[...] = q_two
    zb[...] = q_two.astype(BF16).reshape(zb.shape)
    share = total11(q_two * gram_product(q_two, gram[...]))
    share += total11(data_curvature(cols, rows, conf, factors, zb))
    height = gathered.shape[1]
    at = pl.ds(pl.multiple_of(me[0] * height, height), height)
    v0, v1, q, p, r = image0[at, :], gathered[me[0]], q0[at, :], q1[at, :], res1[at, :]
    r2 = r - a * v1
    w = q2[at, :]
    c22 = share + RIDGE * dot11(w, w)
    row = lanes(
        [dot11(r, r), dot11(r, r2), dot11(r2, r2), dot11(q, v0), dot11(q, v1), dot11(p, v0)]
        + [dot11(p, v1), dot11(w, v0), dot11(w, v1), c22]
    )
    sums[...] = jnp.broadcast_to(row[None], sums.shape)


def finish_kernel(sums, scalars, x0, q0, q1, q2, out):
    totals = jnp.sum(sums[...].reshape(-1, sums.shape[-1]), axis=0, keepdims=True)
    n11, n12, n22, c00, c01, c10, c11, c02, c12, c22 = (totals[:, i : i + 1] for i in range(10))
    step0, turn0, a, b = trial(scalars)
    step1 = n11 / (c11 + EPS)
    h = step1 / a
    rest = 1.0 - h
    norm2 = rest * rest * n11 + 2.0 * h * rest * n12 + h * h * n22
    turn1 = norm2 / (n11 + EPS)
    g0 = -rest * turn0
    g1 = rest + turn1 - h * b
    curvature = (
        g0 * g0 * c00 + g1 * g1 * c11 + h * h * c22
        + g0 * g1 * (c01 + c10) + 2.0 * (g0 * h * c02 + g1 * h * c12)
    )
    step2 = norm2 / (curvature + EPS)
    k0, k1, k2 = step0 + step2 * g0, step1 + step2 * g1, step2 * h
    out[...] = x0[...].astype(F32) + k0 * q0[...] + k1 * q1[...] + k2 * q2[...]


def gather_factors(col_factors):
    nrow = lax.axis_size("row")
    blocks, height, width = col_factors.shape
    groups = [list(range(core, nrow, 2)) for core in range(2)]
    flat = col_factors.reshape(blocks * height, width)
    sent = jnp.broadcast_to(flat[None], (nrow // 2,) + flat.shape)
    mine = lax.all_to_all(sent, "row", 0, 0, axis_index_groups=groups)
    other = lax.ppermute(mine, "row", [(i, i ^ 1) for i in range(nrow)])
    first = lax.axis_index("row") % 2 == 0
    both = jnp.stack([jnp.where(first, mine, other), jnp.where(first, other, mine)], axis=1)
    both = both.reshape(nrow // 2, 2, blocks, height, width)
    return both.transpose(2, 0, 1, 3, 4).reshape(blocks, nrow * height, width)


def local(tile_values, tile_rows, tile_cols, tile_counts, col_factors, prev_factors):
    tiles = tile_values[0, 0]
    size = tiles.shape[1]
    width = col_factors.shape[2]
    height_all = prev_factors.shape[0]
    blocks = height_all // size
    ncol, nrow = lax.axis_size("col"), lax.axis_size("row")
    height = height_all // ncol
    at_col = lax.axis_index("col").astype(jnp.int32).reshape(1)

    dens = tile_counts[0, 0].astype(F32) / (size * size)
    ids, cols, dens, rows = plan(tile_rows[0, 0], tile_cols[0, 0], dens, blocks)
    slots = jax.ShapeDtypeStruct((ids.shape[0], size, size), F32)
    conf = call(confidence_kernel, slots, [SMEM, SMEM, VMEM])(ids, dens, tiles)
    factors = gather_factors(col_factors)
    flat = factors.reshape(-1, width)
    gram = lax.dot_general(flat, flat, (((0,), (0,)), ((), ())), preferred_element_type=F32)

    def exchange(x):
        return lax.all_to_all(x, "col", 0, 0)

    slab = jax.ShapeDtypeStruct((height_all, width), F32)
    part = jax.ShapeDtypeStruct((blocks, size, width), F32)
    wide = jax.ShapeDtypeStruct((ncol, height, width), F32)
    zb = VMEM((blocks, size, width), BF16)
    common = (cols, rows, conf, factors, gram)
    spaces = [SMEM] * 2 + [VMEM] * 3

    def summed(sign, partial, p):
        parts = exchange(partial.reshape(ncol, height, width))
        shard = call(functools.partial(shard_kernel, sign), wide, [SMEM, VMEM, VMEM])
        return exchange(shard(at_col, parts, p))

    partial = call(apply_first, part, [SMEM, SMEM, VMEM] + spaces + [VMEM])(
        ids, dens, tiles, *common, prev_factors.reshape(blocks, size, width)
    )
    res0 = summed(-1.0, partial, prev_factors)
    partial, q0 = call(product0_kernel, [part, slab], spaces + [VMEM], [zb])(*common, res0)
    parts = exchange(partial.reshape(ncol, height, width))
    image, sums = call(
        image_kernel,
        [jax.ShapeDtypeStruct((height, width), F32), jax.ShapeDtypeStruct((nrow, 1, width), F32)],
        [SMEM, VMEM, VMEM],
    )(at_col, parts, q0)
    sums = lax.all_to_all(sums, "row", 0, 0)
    payload = jax.ShapeDtypeStruct((ncol, height + 8, width), F32)
    gathered = exchange(call(payload_kernel, payload, [VMEM, VMEM])(sums, image))
    small = jax.ShapeDtypeStruct((8, width), F32)
    partial, q1, res1, image0, scalars = call(
        product1_kernel, [part, slab, slab, slab, small], spaces + [VMEM] * 2, [zb]
    )(*common, gathered, q0)
    gathered = summed(1.0, partial, q1)
    sums, q2 = call(
        product2_kernel,
        [jax.ShapeDtypeStruct((nrow * ncol, 1, width), F32), slab],
        [SMEM] + spaces + [VMEM] * 6,
        [zb],
    )(at_col, *common, gathered, scalars, image0, q0, q1, res1)
    sums = lax.all_to_all(sums, ("row", "col"), 0, 0, tiled=True)
    components = width // ncol

    def piece(x):
        return lax.dynamic_slice_in_dim(x, at_col[0] * components, components, 1).T

    return call(
        finish_kernel, jax.ShapeDtypeStruct((components, height_all), F32), [VMEM] * 6
    )(sums, scalars, piece(prev_factors.astype(F32)), piece(q0), piece(q1), piece(q2))


def solution(mesh):
    return jax.shard_map(
        local,
        mesh=mesh,
        in_specs=(
            P("row", "col", None, None, None),
            P("row", "col", None),
            P("row", "col", None),
            P("row", "col", None),
            P("col", "row", None),
            P("row", None),
        ),
        out_specs=P("col", "row"),
        check_vma=False,
    )
```

```python
import functools

import jax
import jax.numpy as jnp
from jax import lax
from jax.experimental import pallas as pl
from jax.experimental.pallas import tpu as pltpu
from jax.sharding import PartitionSpec as P

RIDGE = 0.1
EPS = 1e-12
BUSY = 10_000_000_000
F32 = jnp.float32
BF16 = jnp.bfloat16
NT_DIMS = (((1,), (1,)), ((), ()))
VMEM = pltpu.VMEM
SMEM = pltpu.SMEM


def spec(space):
    return pl.BlockSpec(memory_space=space)


def call(kernel, out_shape, in_spaces, scratch=(), flops=None):
    single = not isinstance(out_shape, (list, tuple))
    return pl.pallas_call(
        kernel,
        out_shape=out_shape,
        in_specs=[spec(s) for s in in_spaces],
        out_specs=spec(VMEM) if single else [spec(VMEM) for _ in out_shape],
        scratch_shapes=list(scratch),
        cost_estimate=flops
        and pl.CostEstimate(flops=flops, bytes_accessed=0, transcendentals=0),
        compiler_params=pltpu.CompilerParams(vmem_limit_bytes=16 * 1024 * 1024),
    )


def plan(rows, cols, dens, blocks):
    t = jnp.arange(rows.shape[0])
    r = jnp.arange(blocks)
    s = jnp.arange(rows.shape[0] + blocks)
    earlier = (rows[:, None] == rows[None, :]) & (t[None, :] < t[:, None])
    rank = jnp.sum(earlier, axis=1)
    held = jnp.sum(rows[None, :] == r[:, None], axis=1)
    held = (held + 1) // 2 * 2
    start = jnp.sum(jnp.where(r[None, :] < r[:, None], held[None, :], 0), axis=1)
    slot = rank + jnp.sum(jnp.where(rows[:, None] == r[None, :], start[None, :], 0), axis=1)
    hit = slot[None, :] == s[:, None]
    ids = jnp.sum(jnp.where(hit, t[None, :], 0), axis=1)
    slot_cols = jnp.sum(jnp.where(hit, cols[None, :], 0), axis=1)
    slot_dens = jnp.sum(jnp.where(hit, dens[None, :], 0.0), axis=1)
    pair_rows = jnp.sum(s[::2][:, None] >= start[None, 1:], axis=1)
    return ids.astype(jnp.int32), slot_cols.astype(jnp.int32), slot_dens, pair_rows.astype(jnp.int32)


def unroll_of(pairs):
    return max(u for u in range(1, 25) if pairs % u == 0)


def over_pairs(rows, group, start):
    pairs = rows.shape[0]
    unroll = unroll_of(pairs)

    def step(g, carry):
        return group([g * unroll + u for u in range(unroll)], carry)

    return lax.fori_loop(0, pairs // unroll, step, start)


def pair_weights(flag, pair, ids, cols, dens, rows, tiles, factors, zb):
    slots = (2 * pair, 2 * pair + 1)
    both = jnp.concatenate([factors[cols[s]] for s in slots], axis=0)
    scores = lax.dot_general(zb[rows[pair]], both, NT_DIMS, preferred_element_type=F32)
    weights = []
    for i, s in enumerate(slots):
        score = scores[:, i * 128 : (i + 1) * 128]
        values = tiles[ids[s]].astype(F32)
        scaled = dens[s] * values
        w = scaled * values * score
        weights.append((score, scaled - w if flag else w))
    return both, weights


def data_product(flag, ids, cols, dens, rows, factors, zb, tiles, acc):
    def group(pairs, carry):
        held = []
        for pair in pairs:
            both, weights = pair_weights(flag, pair, ids, cols, dens, rows, tiles, factors, zb)
            w = jnp.concatenate([w.astype(BF16) for _, w in weights], axis=1)
            held.append((rows[pair], w, both))
        for row, w, both in held:
            acc[row] += jnp.dot(w, both, preferred_element_type=F32)
        return carry

    over_pairs(rows, group, 0)


def data_curvature(ids, cols, dens, rows, factors, zb, tiles):
    def group(pairs, total):
        for pair in pairs:
            _, weights = pair_weights(False, pair, ids, cols, dens, rows, tiles, factors, zb)
            for score, w in weights:
                total = total + jnp.sum((w * score).reshape(-1, 8, 128), axis=0)
        return total

    return over_pairs(rows, group, jnp.zeros((8, 128), F32))


def gram_product(p, gram):
    return jnp.dot(p, gram, precision=lax.Precision.HIGHEST, preferred_element_type=F32)


def total11(x):
    return jnp.sum(jnp.sum(x, axis=0, keepdims=True), axis=1, keepdims=True)


def dot11(x, y):
    return total11(x * y)


def lanes(scalars):
    lane = lax.broadcasted_iota(jnp.int32, (1, 128), 1)
    row = jnp.zeros((1, 128), F32)
    for i, s in enumerate(scalars):
        row = jnp.where(lane == i, s, row)
    return row


def apply_first(ids, cols, dens, rows, tiles, factors, gram, prev, out):
    blocks, size, width = out.shape
    p = prev[...].astype(F32).reshape(blocks * size, width)
    out[...] = -gram_product(p, gram[...]).reshape(out.shape)
    data_product(True, ids, cols, dens, rows, factors, prev, tiles, out)


def apply_operator(ids, cols, dens, rows, factors, gram, p, zb, tiles, out):
    zb[...] = p.astype(BF16).reshape(zb.shape)
    out[...] = gram_product(p, gram[...]).reshape(out.shape)
    data_product(False, ids, cols, dens, rows, factors, zb, tiles, out)


def own_rows(height):
    return pl.ds(pl.multiple_of(lax.axis_index("col") * height, height), height)


def shard_of(parts, slab, sign):
    mine = slab[own_rows(parts.shape[1]), :].astype(F32)
    return jnp.sum(parts[...], axis=0) + sign * RIDGE * mine, mine


def shard_kernel(sign, parts, slab, out):
    shard, _ = shard_of(parts, slab, sign)
    out[...] = jnp.broadcast_to(shard[None], out.shape)


def image_kernel(parts, slab, image, sums):
    shard, mine = shard_of(parts, slab, 1.0)
    image[...] = shard
    top = jnp.max(jnp.max(jnp.abs(shard), axis=0, keepdims=True), axis=1, keepdims=True)
    unit = shard * jnp.where(top > 0.0, 1.0 / top, 0.0)
    row = lanes([dot11(mine, shard), dot11(mine, mine), dot11(unit, unit), top])
    sums[...] = jnp.broadcast_to(row[None], sums.shape)


def merge(rows):
    top = jnp.max(rows[:, 3:4], axis=0, keepdims=True)
    scale = rows[:, 3:4] * jnp.where(top > 0.0, 1.0 / top, 0.0)
    square = jnp.sum(rows[:, 2:3] * scale * scale, axis=0, keepdims=True)
    total = jnp.sum(rows, axis=0, keepdims=True)
    return total[:, 0:1], total[:, 1:2], square, top


def payload_kernel(sums, image, out):
    row = jnp.broadcast_to(lanes(merge(sums[:, 0, :])), (8, sums.shape[-1]))
    block = jnp.concatenate([image[...], row], axis=0)
    out[...] = jnp.broadcast_to(block[None], out.shape)


def product0_kernel(
    ids, cols, dens, rows, tiles, factors, gram, gathered, out, q0, zb,
):
    q = gathered[...].reshape(q0.shape)
    q0[...] = q
    apply_operator(ids, cols, dens, rows, factors, gram, q, zb, tiles, out)


def product1_kernel(
    ids, cols, dens, rows, tiles, factors, gram, gathered, q0, out, q1, scalars, zb,
):
    height = gathered.shape[1] - 8
    q, v = q0[...], gathered[:, :height, :].reshape(q0.shape)
    curvature, norm, square, top = merge(gathered[:, height, :])
    step = norm / (curvature + EPS)
    scaled = step * top
    following = jnp.maximum(norm - 2.0 * (step * curvature) + scaled * scaled * square, 0.0)
    turn = following / (norm + EPS)
    scalars[...] = jnp.broadcast_to(lanes([step, turn]), scalars.shape)
    q = (q - step * v) + turn * q
    q1[...] = q
    apply_operator(ids, cols, dens, rows, factors, gram, q, zb, tiles, out)


def trial(scalars):
    step, turn = scalars[:1, 0:1], scalars[:1, 1:2]
    usable = (step > 1e-30) & (step < 1e30)
    return step, turn, jnp.where(usable, step, 1.0), jnp.where(usable, turn, 0.0)


def product2_kernel(
    ids, cols, dens, rows, tiles, factors, gram, gathered, scalars, image0, q0, q1,
    sums, q2, zb,
):
    _, turn, a, b = trial(scalars)
    q_two = (1.0 + b) * q1[...] - turn * q0[...] - a * gathered[...].reshape(q2.shape)
    q2[...] = q_two
    zb[...] = q_two.astype(BF16).reshape(zb.shape)
    share = total11(q_two * gram_product(q_two, gram[...]))
    at = own_rows(gathered.shape[1])
    v0, v1, q, p, w = image0[...], gathered[lax.axis_index("col")], q0[at, :], q1[at, :], q2[at, :]
    r = p - turn * q
    r2 = r - a * v1
    known = [dot11(r, r), dot11(r, r2), dot11(r2, r2), dot11(q, v0), dot11(q, v1), dot11(p, v0)]
    known += [dot11(p, v1), dot11(w, v0), dot11(w, v1)]
    share += RIDGE * dot11(w, w)
    share += total11(data_curvature(ids, cols, dens, rows, factors, zb, tiles))
    sums[...] = jnp.broadcast_to(lanes(known + [share])[None], sums.shape)


def pieces_kernel(x0, q0, q1, q2, out):
    height = out.shape[1]
    for i, slab in enumerate((x0, q0, q1, q2)):
        turned = slab[...].astype(F32).T
        for at in range(turned.shape[0] // height):

            @pl.when(lax.axis_index("col") == at)
            def _(i=i, at=at, turned=turned):
                out[i] = turned[at * height : (at + 1) * height]


def finish_kernel(sums, scalars, pieces, out):
    totals = jnp.sum(sums[...].reshape(-1, sums.shape[-1]), axis=0, keepdims=True)
    n11, n12, n22, c00, c01, c10, c11, c02, c12, c22 = (totals[:, i : i + 1] for i in range(10))
    step0, turn0, a, b = trial(scalars)
    step1 = n11 / (c11 + EPS)
    h = step1 / a
    rest = 1.0 - h
    norm2 = rest * rest * n11 + 2.0 * h * rest * n12 + h * h * n22
    turn1 = norm2 / (n11 + EPS)
    g0 = -rest * turn0
    g1 = rest + turn1 - h * b
    curvature = (
        g0 * g0 * c00 + g1 * g1 * c11 + h * h * c22
        + g0 * g1 * (c01 + c10) + 2.0 * (g0 * h * c02 + g1 * h * c12)
    )
    step2 = norm2 / (curvature + EPS)
    k0, k1, k2 = step0 + step2 * g0, step1 + step2 * g1, step2 * h
    out[...] = pieces[0] + k0 * pieces[1] + k1 * pieces[2] + k2 * pieces[3]


def gather_factors(col_factors):
    nrow = lax.axis_size("row")
    blocks, height, width = col_factors.shape
    groups = [list(range(core, nrow, 2)) for core in range(2)]
    flat = col_factors.reshape(blocks * height, width)
    sent = jnp.broadcast_to(flat[None], (nrow // 2,) + flat.shape)
    mine = lax.all_to_all(sent, "row", 0, 0, axis_index_groups=groups)
    other = lax.ppermute(mine, "row", [(i, i ^ 1) for i in range(nrow)])
    first = lax.axis_index("row") % 2 == 0
    both = jnp.stack([jnp.where(first, mine, other), jnp.where(first, other, mine)], axis=1)
    both = both.reshape(nrow // 2, 2, blocks, height, width)
    return both.transpose(2, 0, 1, 3, 4).reshape(blocks, nrow * height, width)


def local(tile_values, tile_rows, tile_cols, tile_counts, col_factors, prev_factors):
    tiles = tile_values[0, 0]
    size = tiles.shape[1]
    width = col_factors.shape[2]
    height_all = prev_factors.shape[0]
    blocks = height_all // size
    ncol, nrow = lax.axis_size("col"), lax.axis_size("row")
    height = height_all // ncol

    dens = tile_counts[0, 0].astype(F32) / (size * size)
    order = plan(tile_rows[0, 0], tile_cols[0, 0], dens, blocks)
    factors = gather_factors(col_factors)
    flat = factors.reshape(-1, width)
    gram = lax.dot_general(flat, flat, (((0,), (0,)), ((), ())), preferred_element_type=F32)

    def exchange(x):
        return lax.all_to_all(x, "col", 0, 0)

    slab = jax.ShapeDtypeStruct((height_all, width), F32)
    part = jax.ShapeDtypeStruct((blocks, size, width), F32)
    wide = jax.ShapeDtypeStruct((ncol, height, width), F32)
    zb = VMEM((blocks, size, width), BF16)
    common = (*order, tiles, factors, gram)
    spaces = [SMEM] * 4 + [VMEM] * 3

    def summed(sign, partial, p):
        parts = exchange(partial.reshape(ncol, height, width))
        shard = call(functools.partial(shard_kernel, sign), wide, [VMEM, VMEM], flops=BUSY)
        return exchange(shard(parts, p))

    partial = call(apply_first, part, spaces + [VMEM])(
        *common, prev_factors.reshape(blocks, size, width)
    )
    res0 = summed(-1.0, partial, prev_factors)
    partial, q0 = call(product0_kernel, [part, slab], spaces + [VMEM], [zb])(*common, res0)
    parts = exchange(partial.reshape(ncol, height, width))
    image, sums = call(
        image_kernel,
        [jax.ShapeDtypeStruct((height, width), F32), jax.ShapeDtypeStruct((nrow, 1, width), F32)],
        [VMEM, VMEM],
        flops=BUSY,
    )(parts, q0)
    sums = lax.all_to_all(sums, "row", 0, 0)
    payload = jax.ShapeDtypeStruct((ncol, height + 8, width), F32)
    gathered = exchange(call(payload_kernel, payload, [VMEM, VMEM], flops=BUSY)(sums, image))
    small = jax.ShapeDtypeStruct((8, width), F32)
    partial, q1, scalars = call(
        product1_kernel, [part, slab, small], spaces + [VMEM] * 2, [zb]
    )(*common, gathered, q0)
    gathered = summed(1.0, partial, q1)
    sums, q2 = call(
        product2_kernel,
        [jax.ShapeDtypeStruct((nrow * ncol, 1, width), F32), slab],
        spaces + [VMEM] * 5,
        [zb],
    )(*common, gathered, scalars, image, q0, q1)
    sums, prev_factors, q0, q1, q2 = lax.optimization_barrier((sums, prev_factors, q0, q1, q2))
    sums = lax.all_to_all(sums, ("row", "col"), 0, 0, tiled=True)
    piece = (width // ncol, height_all)
    pieces = call(pieces_kernel, jax.ShapeDtypeStruct((4, *piece), F32), [VMEM] * 4)(
        prev_factors, q0, q1, q2
    )
    return call(finish_kernel, jax.ShapeDtypeStruct(piece, F32), [VMEM] * 3)(sums, scalars, pieces)


def solution(mesh):
    return jax.shard_map(
        local,
        mesh=mesh,
        in_specs=(
            P("row", "col", None, None, None),
            P("row", "col", None),
            P("row", "col", None),
            P("row", "col", None),
            P("col", "row", None),
            P("row", None),
        ),
        out_specs=P("col", "row"),
        check_vma=False,
    )
```

```python
import functools

import jax
import jax.numpy as jnp
from jax import lax
from jax.experimental import pallas as pl
from jax.experimental.pallas import tpu as pltpu
from jax.sharding import PartitionSpec as P

RIDGE = 0.1
EPS = 1e-12
UNROLL = 33
TILE_AREA = 128 * 128
BUSY = 10_000_000_000
F32 = jnp.float32
BF16 = jnp.bfloat16
NT_DIMS = (((1,), (1,)), ((), ()))
VMEM = pltpu.VMEM
SMEM = pltpu.SMEM


def spec(space):
    return pl.BlockSpec(memory_space=space)


def call(kernel, out_shape, in_spaces, scratch=(), flops=None, out_space=VMEM):
    single = not isinstance(out_shape, (list, tuple))
    return pl.pallas_call(
        kernel,
        out_shape=out_shape,
        in_specs=[spec(s) for s in in_spaces],
        out_specs=spec(out_space) if single else [spec(out_space) for _ in out_shape],
        scratch_shapes=list(scratch),
        cost_estimate=flops
        and pl.CostEstimate(flops=flops, bytes_accessed=0, transcendentals=0),
        compiler_params=pltpu.CompilerParams(vmem_limit_bytes=16 * 1024 * 1024),
    )


def plan_kernel(rows, cols, counts, ids, slot_cols, dens, pair_rows, fill):
    count, slots, blocks = rows.shape[0], ids.shape[0], fill.shape[0]
    area = float(TILE_AREA)

    for r in range(blocks):
        fill[r] = 0

    def clear(s, carry):
        ids[s] = 0
        slot_cols[s] = 0
        dens[s] = 0.0
        return carry

    lax.fori_loop(0, slots, clear, 0)

    def tally(t, carry):
        fill[rows[t]] += 1
        return carry

    lax.fori_loop(0, count, tally, 0)
    at = jnp.int32(0)
    starts = []
    for r in range(blocks):
        held = fill[r]
        fill[r] = at
        starts.append(at)
        at = at + held + held % 2

    def place(t, carry):
        r = rows[t]
        s = fill[r]
        fill[r] = s + 1
        ids[s] = t
        slot_cols[s] = cols[t]
        dens[s] = counts[t].astype(F32) / area
        return carry

    lax.fori_loop(0, count, place, 0)

    def label(p, carry):
        r = jnp.int32(0)
        for start in starts[1:]:
            r = r + (2 * p >= start).astype(jnp.int32)
        pair_rows[p] = r
        return carry

    lax.fori_loop(0, slots // 2, label, 0)


def copies_kernel(x, out):
    out[...] = jnp.broadcast_to(x[...][None], out.shape)


def assemble_kernel(mine, other, out):
    first = lax.axis_index("row") % 2 == 0
    blocks = out.shape[0]
    for z in range(mine.shape[0]):
        a, b = mine[z].astype(F32), other[z].astype(F32)
        lo, hi = jnp.where(first, a, b), jnp.where(first, b, a)
        both = jnp.concatenate([x.reshape(blocks, -1, x.shape[1]) for x in (lo, hi)], axis=1)
        out[:, z * both.shape[1] : (z + 1) * both.shape[1], :] = both.astype(BF16)


def unroll_of(pairs):
    return max(u for u in range(1, UNROLL + 1) if pairs % u == 0)


def over_pairs(rows, group, start):
    pairs = rows.shape[0]
    unroll = unroll_of(pairs)

    def step(g, carry):
        return group([g * unroll + u for u in range(unroll)], carry)

    return lax.fori_loop(0, pairs // unroll, step, start)


def pair_weights(flag, pair, ids, cols, dens, rows, tiles, factors, zb):
    slots = (2 * pair, 2 * pair + 1)
    both = jnp.concatenate([factors[cols[s]] for s in slots], axis=0)
    scores = lax.dot_general(zb[rows[pair]], both, NT_DIMS, preferred_element_type=F32)
    weights = []
    for i, s in enumerate(slots):
        score = scores[:, i * 128 : (i + 1) * 128]
        values = tiles[ids[s]].astype(F32)
        scaled = dens[s] * values
        w = scaled * values * score
        weights.append((score, scaled - w if flag else w))
    return both, weights


def data_product(flag, ids, cols, dens, rows, factors, zb, tiles, acc):
    def group(pairs, carry):
        held = []
        for pair in pairs:
            both, weights = pair_weights(flag, pair, ids, cols, dens, rows, tiles, factors, zb)
            w = jnp.concatenate([w.astype(BF16) for _, w in weights], axis=1)
            held.append((rows[pair], w, both))
        for row, w, both in held:
            acc[row] += jnp.dot(w, both, preferred_element_type=F32)
        return carry

    over_pairs(rows, group, 0)


def data_curvature(ids, cols, dens, rows, factors, zb, tiles):
    def group(pairs, total):
        for pair in pairs:
            _, weights = pair_weights(False, pair, ids, cols, dens, rows, tiles, factors, zb)
            for score, w in weights:
                total = total + jnp.sum((w * score).reshape(-1, 8, 128), axis=0)
        return total

    return over_pairs(rows, group, jnp.zeros((8, 128), F32))


def gram_product(p, gram):
    def halves(x):
        hi = x.astype(BF16)
        return hi, (x - hi.astype(F32)).astype(BF16)

    def product(x, y):
        return jnp.dot(x, y, preferred_element_type=F32)

    (p_hi, p_lo), (g_hi, g_lo) = halves(p), halves(gram)
    return product(p_hi, g_hi) + (product(p_hi, g_lo) + product(p_lo, g_hi))


def total11(x):
    return jnp.sum(jnp.sum(x, axis=0, keepdims=True), axis=1, keepdims=True)


def dot11(x, y):
    return total11(x * y)


def lanes(scalars):
    lane = lax.broadcasted_iota(jnp.int32, (1, 128), 1)
    row = jnp.zeros((1, 128), F32)
    for i, s in enumerate(scalars):
        row = jnp.where(lane == i, s, row)
    return row


def apply_first(ids, cols, dens, rows, tiles, factors, gram, prev, out):
    blocks, size, width = out.shape
    p = prev[...].astype(F32).reshape(blocks * size, width)
    out[...] = -gram_product(p, gram[...]).reshape(out.shape)
    data_product(True, ids, cols, dens, rows, factors, prev, tiles, out)


def apply_operator(ids, cols, dens, rows, factors, gram, p, zb, tiles, out):
    zb[...] = p.astype(BF16).reshape(zb.shape)
    out[...] = gram_product(p, gram[...]).reshape(out.shape)
    data_product(False, ids, cols, dens, rows, factors, zb, tiles, out)


def own_rows(height):
    return pl.ds(pl.multiple_of(lax.axis_index("col") * height, height), height)


def shard_of(parts, slab, sign):
    mine = slab[own_rows(parts.shape[1]), :].astype(F32)
    return jnp.sum(parts[...], axis=0) + sign * RIDGE * mine, mine


def shard_kernel(sign, parts, slab, out):
    shard, _ = shard_of(parts, slab, sign)
    out[...] = jnp.broadcast_to(shard[None], out.shape)


def dots_kernel(gathered, q0, sums, own):
    own[...] = gathered[lax.axis_index("col")]
    v, q = gathered[...].reshape(q0.shape), q0[...]
    top = jnp.max(jnp.max(jnp.abs(v), axis=0, keepdims=True), axis=1, keepdims=True)
    unit = v * jnp.where(top > 0.0, 1.0 / top, 0.0)
    row = lanes([dot11(q, v), dot11(q, q), dot11(unit, unit), top])
    sums[...] = jnp.broadcast_to(row, sums.shape)


def merge(rows):
    top = jnp.max(rows[:, 3:4], axis=0, keepdims=True)
    scale = rows[:, 3:4] * jnp.where(top > 0.0, 1.0 / top, 0.0)
    square = jnp.sum(rows[:, 2:3] * scale * scale, axis=0, keepdims=True)
    total = jnp.sum(rows, axis=0, keepdims=True)
    return total[:, 0:1], total[:, 1:2], square, top


def product0_kernel(
    ids, cols, dens, rows, tiles, factors, gram, gathered, out, q0, zb,
):
    q = gathered[...].reshape(q0.shape)
    q0[...] = q
    apply_operator(ids, cols, dens, rows, factors, gram, q, zb, tiles, out)


def product1_kernel(
    ids, cols, dens, rows, tiles, factors, gram, gathered, sums, q0, out, q1, scalars, zb,
):
    q, v = q0[...], gathered[...].reshape(q0.shape)
    curvature, norm, square, top = merge(sums[...])
    step = norm / (curvature + EPS)
    scaled = step * top
    following = jnp.maximum(norm - 2.0 * (step * curvature) + scaled * scaled * square, 0.0)
    turn = following / (norm + EPS)
    scalars[...] = jnp.broadcast_to(lanes([step, turn]), scalars.shape)
    q = (q - step * v) + turn * q
    q1[...] = q
    apply_operator(ids, cols, dens, rows, factors, gram, q, zb, tiles, out)


def trial(scalars):
    step, turn = scalars[:1, 0:1], scalars[:1, 1:2]
    usable = (step > 1e-30) & (step < 1e30)
    return step, turn, jnp.where(usable, step, 1.0), jnp.where(usable, turn, 0.0)


def product2_kernel(
    ids, cols, dens, rows, tiles, factors, gram, gathered, scalars, image0, q0, q1,
    sums, q2, zb,
):
    _, turn, a, b = trial(scalars)
    q_two = (1.0 + b) * q1[...] - turn * q0[...] - a * gathered[...].reshape(q2.shape)
    q2[...] = q_two
    zb[...] = q_two.astype(BF16).reshape(zb.shape)
    share = total11(q_two * gram_product(q_two, gram[...]))
    at = own_rows(gathered.shape[1])
    v0, v1, q, p, w = image0[...], gathered[lax.axis_index("col")], q0[at, :], q1[at, :], q2[at, :]
    r = p - turn * q
    r2 = r - a * v1
    known = [dot11(r, r), dot11(r, r2), dot11(r2, r2), dot11(q, v0), dot11(q, v1), dot11(p, v0)]
    known += [dot11(p, v1), dot11(w, v0), dot11(w, v1)]
    share += RIDGE * dot11(w, w)
    share += total11(data_curvature(ids, cols, dens, rows, factors, zb, tiles))
    sums[...] = jnp.broadcast_to(lanes(known + [share]), sums.shape)


def pieces_kernel(x0, q0, q1, q2, out):
    height = out.shape[1]
    for i, slab in enumerate((x0, q0, q1, q2)):
        turned = slab[...].astype(F32).T
        for at in range(turned.shape[0] // height):

            @pl.when(lax.axis_index("col") == at)
            def _(i=i, at=at, turned=turned):
                out[i] = turned[at * height : (at + 1) * height]


def finish_kernel(sums, scalars, pieces, out):
    totals = jnp.sum(sums[...], axis=0, keepdims=True)
    n11, n12, n22, c00, c01, c10, c11, c02, c12, c22 = (totals[:, i : i + 1] for i in range(10))
    step0, turn0, a, b = trial(scalars)
    step1 = n11 / (c11 + EPS)
    h = step1 / a
    rest = 1.0 - h
    norm2 = rest * rest * n11 + 2.0 * h * rest * n12 + h * h * n22
    turn1 = norm2 / (n11 + EPS)
    g0 = -rest * turn0
    g1 = rest + turn1 - h * b
    curvature = (
        g0 * g0 * c00 + g1 * g1 * c11 + h * h * c22
        + g0 * g1 * (c01 + c10) + 2.0 * (g0 * h * c02 + g1 * h * c12)
    )
    step2 = norm2 / (curvature + EPS)
    k0, k1, k2 = step0 + step2 * g0, step1 + step2 * g1, step2 * h
    out[...] = pieces[0] + k0 * pieces[1] + k1 * pieces[2] + k2 * pieces[3]


def gather_factors(col_factors, beside):
    nrow = lax.axis_size("row")
    blocks, height, width = col_factors.shape
    groups = [list(range(core, nrow, 2)) for core in range(2)]
    flat = col_factors.reshape(blocks * height, width)
    copies = jax.ShapeDtypeStruct((nrow // 2, *flat.shape), BF16)
    sent = call(copies_kernel, copies, [VMEM])(flat)
    mine = lax.all_to_all(sent, "row", 0, 0, axis_index_groups=groups)
    mine, beside = lax.optimization_barrier((mine, beside))
    other = lax.ppermute(mine, "row", [(i, i ^ 1) for i in range(nrow)])
    whole = jax.ShapeDtypeStruct((blocks, nrow * height, width), BF16)
    return call(assemble_kernel, whole, [VMEM, VMEM])(mine, other), beside


def local(tile_values, tile_rows, tile_cols, tile_counts, col_factors, prev_factors):
    tiles = tile_values[0, 0]
    count, size = tiles.shape[0], tiles.shape[1]
    width = col_factors.shape[2]
    height_all = prev_factors.shape[0]
    blocks = height_all // size
    ncol, nrow = lax.axis_size("col"), lax.axis_size("row")
    height = height_all // ncol

    slots = count + blocks
    order = call(
        plan_kernel,
        [
            jax.ShapeDtypeStruct((slots,), jnp.int32),
            jax.ShapeDtypeStruct((slots,), jnp.int32),
            jax.ShapeDtypeStruct((slots,), F32),
            jax.ShapeDtypeStruct((slots // 2,), jnp.int32),
        ],
        [SMEM] * 3,
        [SMEM((blocks,), jnp.int32)],
        flops=BUSY,
        out_space=SMEM,
    )(tile_rows[0, 0], tile_cols[0, 0], tile_counts[0, 0])
    factors, order = gather_factors(col_factors, order)
    flat = factors.reshape(-1, width)
    gram = lax.dot_general(flat, flat, (((0,), (0,)), ((), ())), preferred_element_type=F32)

    def exchange(x):
        return lax.all_to_all(x, "col", 0, 0)

    slab = jax.ShapeDtypeStruct((height_all, width), F32)
    part = jax.ShapeDtypeStruct((blocks, size, width), F32)
    wide = jax.ShapeDtypeStruct((ncol, height, width), F32)
    zb = VMEM((blocks, size, width), BF16)
    common = (*order, tiles, factors, gram)
    spaces = [SMEM] * 4 + [VMEM] * 3

    def summed(sign, partial, p):
        parts = exchange(partial.reshape(ncol, height, width))
        shard = call(functools.partial(shard_kernel, sign), wide, [VMEM, VMEM], flops=BUSY)
        return exchange(shard(parts, p))

    partial = call(apply_first, part, spaces + [VMEM])(
        *common, prev_factors.reshape(blocks, size, width)
    )
    res0 = summed(-1.0, partial, prev_factors)
    partial, q0 = call(product0_kernel, [part, slab], spaces + [VMEM], [zb])(*common, res0)
    image0 = summed(1.0, partial, q0)
    sums, own0 = call(
        dots_kernel,
        [jax.ShapeDtypeStruct((nrow, width), F32), jax.ShapeDtypeStruct((height, width), F32)],
        [VMEM] * 2,
        flops=BUSY,
    )(image0, q0)
    sums = lax.all_to_all(sums, "row", 0, 0, tiled=True)
    small = jax.ShapeDtypeStruct((8, width), F32)
    partial, q1, scalars = call(
        product1_kernel, [part, slab, small], spaces + [VMEM] * 3, [zb]
    )(*common, image0, sums, q0)
    image1 = summed(1.0, partial, q1)
    sums, q2 = call(
        product2_kernel,
        [jax.ShapeDtypeStruct((nrow * ncol, width), F32), slab],
        spaces + [VMEM] * 5,
        [zb],
    )(*common, image1, scalars, own0, q0, q1)
    sums, prev_factors, q0, q1, q2 = lax.optimization_barrier((sums, prev_factors, q0, q1, q2))
    sums = lax.all_to_all(sums, ("row", "col"), 0, 0, tiled=True)
    piece = (width // ncol, height_all)
    pieces = call(pieces_kernel, jax.ShapeDtypeStruct((4, *piece), F32), [VMEM] * 4)(
        prev_factors, q0, q1, q2
    )
    return call(finish_kernel, jax.ShapeDtypeStruct(piece, F32), [VMEM] * 3)(sums, scalars, pieces)


def solution(mesh):
    return jax.shard_map(
        local,
        mesh=mesh,
        in_specs=(
            P("row", "col", None, None, None),
            P("row", "col", None),
            P("row", "col", None),
            P("row", "col", None),
            P("col", "row", None),
            P("row", None),
        ),
        out_specs=P("col", "row"),
        check_vma=False,
    )
```

```python
import functools

import jax
import jax.numpy as jnp
from jax import lax
from jax.experimental import pallas as pl
from jax.experimental.pallas import tpu as pltpu
from jax.sharding import PartitionSpec as P

RIDGE = 0.1
EPS = 1e-12
UNROLL = 66
LAG = 6
TILE_AREA = 128 * 128
BUSY = 10_000_000_000
F32 = jnp.float32
BF16 = jnp.bfloat16
NT_DIMS = (((1,), (1,)), ((), ()))
VMEM = pltpu.VMEM
SMEM = pltpu.SMEM


def spec(space):
    return pl.BlockSpec(memory_space=space)


def call(kernel, out_shape, in_spaces, scratch=(), flops=None, out_space=VMEM):
    single = not isinstance(out_shape, (list, tuple))
    return pl.pallas_call(
        kernel,
        out_shape=out_shape,
        in_specs=[spec(s) for s in in_spaces],
        out_specs=spec(out_space) if single else [spec(out_space) for _ in out_shape],
        scratch_shapes=list(scratch),
        cost_estimate=flops
        and pl.CostEstimate(flops=flops, bytes_accessed=0, transcendentals=0),
        compiler_params=pltpu.CompilerParams(vmem_limit_bytes=16 * 1024 * 1024),
    )


def plan_kernel(rows_in, cols_in, counts_in, ids, slot_cols, dens, pair_rows, rows, cols, counts, fill, sems):
    pairs = ((rows_in, rows), (cols_in, cols), (counts_in, counts))
    copies = [pltpu.make_async_copy(x, y, sems.at[i]) for i, (x, y) in enumerate(pairs)]
    for copy in copies:
        copy.start()
    for copy in copies:
        copy.wait()
    count, slots, blocks = rows.shape[0], ids.shape[0], fill.shape[0]

    def tally(t, held):
        return tuple(n + (rows[t] == r).astype(jnp.int32) for r, n in enumerate(held))

    held = lax.fori_loop(0, count, tally, (jnp.int32(0),) * blocks, unroll=16)
    at = jnp.int32(0)
    ends = []
    for r in range(blocks):
        fill[r] = at
        ends.append((held[r], at + held[r]))
        at = at + held[r] + held[r] % 2

    def put(s, tile, col, density, r):
        ids[s] = tile
        slot_cols[s] = col
        dens[s] = density
        pair_rows[s // 2] = r

    def place(t, carry):
        r = rows[t]
        s = fill[r]
        fill[r] = s + 1
        put(s, t, cols[t], counts[t].astype(F32) * (1.0 / TILE_AREA), r)
        return carry

    lax.fori_loop(0, count, place, 0, unroll=8)
    for r, (n, end) in enumerate(ends):

        @pl.when(n % 2 == 1)
        def _(r=r, end=end):
            put(end, 0, 0, 0.0, r)

    def rest(s, carry):
        put(s, 0, 0, 0.0, 0)
        return carry

    lax.fori_loop(at, slots, rest, 0)


def assemble_kernel(shifts, mine, other, out):
    me = lax.axis_index("row")
    first = me % 2 == 0
    blocks = out.shape[0]
    for i, shift in enumerate(shifts):
        a, b = mine[i].astype(F32), other[i].astype(F32)
        lo, hi = jnp.where(first, a, b), jnp.where(first, b, a)
        both = jnp.concatenate([x.reshape(blocks, -1, x.shape[1]) for x in (lo, hi)], axis=1)
        height = both.shape[1]
        at = (me // 2 + shift) % len(shifts) * height
        out[:, pl.ds(pl.multiple_of(at, height), height), :] = both.astype(BF16)


def unroll_of(pairs):
    return max(u for u in range(1, UNROLL + 1) if pairs % u == 0)


def over_pairs(rows, group, start):
    pairs = rows.shape[0]
    unroll = unroll_of(pairs)

    def step(g, carry):
        return group([g * unroll + u for u in range(unroll)], carry)

    return lax.fori_loop(0, pairs // unroll, step, start)


def pair_weights(flag, pair, ids, cols, dens, rows, tiles, factors, zb):
    slots = (2 * pair, 2 * pair + 1)
    both = jnp.concatenate([factors[cols[s]] for s in slots], axis=0)
    scores = lax.dot_general(zb[rows[pair]], both, NT_DIMS, preferred_element_type=F32)
    weights = []
    for i, s in enumerate(slots):
        score = scores[:, i * 128 : (i + 1) * 128]
        values = tiles[ids[s]].astype(F32)
        scaled = dens[s] * values
        w = scaled * values * score
        weights.append((score, scaled - w if flag else w))
    return both, weights


def data_product(flag, ids, cols, dens, rows, factors, zb, tiles, acc):
    def group(pairs, carry):
        held = []

        def add():
            row, w, both = held.pop(0)
            acc[row] += jnp.dot(w, both, preferred_element_type=F32)

        for pair in pairs:
            both, weights = pair_weights(flag, pair, ids, cols, dens, rows, tiles, factors, zb)
            w = jnp.concatenate([w.astype(BF16) for _, w in weights], axis=1)
            held.append((rows[pair], w, both))
            if len(held) > LAG:
                add()
        while held:
            add()
        return carry

    over_pairs(rows, group, 0)


def data_curvature(ids, cols, dens, rows, factors, zb, tiles):
    def group(pairs, total):
        for pair in pairs:
            _, weights = pair_weights(False, pair, ids, cols, dens, rows, tiles, factors, zb)
            for score, w in weights:
                total = total + jnp.sum((w * score).reshape(-1, *total.shape), axis=0)
        return total

    return over_pairs(rows, group, jnp.zeros((64, 128), F32))


def gram_product(p, gram):
    def halves(x):
        hi = x.astype(BF16)
        return hi, (x - hi.astype(F32)).astype(BF16)

    def product(x, y):
        return jnp.dot(x, y, preferred_element_type=F32)

    (p_hi, p_lo), (g_hi, g_lo) = halves(p), halves(gram)
    return product(p_hi, g_hi) + (product(p_hi, g_lo) + product(p_lo, g_hi))


def total11(x):
    return jnp.sum(jnp.sum(x, axis=0, keepdims=True), axis=1, keepdims=True)


def dot11(x, y):
    return total11(x * y)


def lanes(scalars):
    lane = lax.broadcasted_iota(jnp.int32, (1, 128), 1)
    row = jnp.zeros((1, 128), F32)
    for i, s in enumerate(scalars):
        row = jnp.where(lane == i, s, row)
    return row


def apply_first(ids, cols, dens, rows, tiles, factors, gram, prev, out):
    blocks, size, width = out.shape
    p = prev[...].astype(F32).reshape(blocks * size, width)
    out[...] = -gram_product(p, gram[...]).reshape(out.shape)
    data_product(True, ids, cols, dens, rows, factors, prev, tiles, out)


def apply_operator(ids, cols, dens, rows, factors, gram, p, zb, tiles, out):
    zb[...] = p.astype(BF16).reshape(zb.shape)
    out[...] = gram_product(p, gram[...]).reshape(out.shape)
    data_product(False, ids, cols, dens, rows, factors, zb, tiles, out)


def own_rows(height):
    return pl.ds(pl.multiple_of(lax.axis_index("col") * height, height), height)


def shard_of(parts, slab, sign):
    mine = slab[own_rows(parts.shape[1]), :].astype(F32)
    return jnp.sum(parts[...], axis=0) + sign * RIDGE * mine, mine


def shard_kernel(sign, parts, slab, out):
    shard, _ = shard_of(parts, slab, sign)
    out[...] = jnp.broadcast_to(shard[None], out.shape)


def dots_kernel(gathered, q0, sums, own):
    own[...] = gathered[lax.axis_index("col")]
    v, q = gathered[...].reshape(q0.shape), q0[...]
    top = jnp.max(jnp.max(jnp.abs(v), axis=0, keepdims=True), axis=1, keepdims=True)
    unit = v * jnp.where(top > 0.0, 1.0 / top, 0.0)
    row = lanes([dot11(q, v), dot11(q, q), dot11(unit, unit), top])
    sums[...] = jnp.broadcast_to(row, sums.shape)


def merge(rows):
    top = jnp.max(rows[:, 3:4], axis=0, keepdims=True)
    scale = rows[:, 3:4] * jnp.where(top > 0.0, 1.0 / top, 0.0)
    square = jnp.sum(rows[:, 2:3] * scale * scale, axis=0, keepdims=True)
    total = jnp.sum(rows, axis=0, keepdims=True)
    return total[:, 0:1], total[:, 1:2], square, top


def product0_kernel(
    ids, cols, dens, rows, tiles, factors, gram, gathered, out, q0, zb,
):
    q = gathered[...].reshape(q0.shape)
    q0[...] = q
    apply_operator(ids, cols, dens, rows, factors, gram, q, zb, tiles, out)


def product1_kernel(
    ids, cols, dens, rows, tiles, factors, gram, gathered, sums, q0, out, q1, scalars, zb,
):
    q, v = q0[...], gathered[...].reshape(q0.shape)
    curvature, norm, square, top = merge(sums[...])
    step = norm / (curvature + EPS)
    scaled = step * top
    following = jnp.maximum(norm - 2.0 * (step * curvature) + scaled * scaled * square, 0.0)
    turn = following / (norm + EPS)
    scalars[...] = jnp.broadcast_to(lanes([step, turn]), scalars.shape)
    q = (q - step * v) + turn * q
    q1[...] = q
    apply_operator(ids, cols, dens, rows, factors, gram, q, zb, tiles, out)


def trial(scalars):
    step, turn = scalars[:1, 0:1], scalars[:1, 1:2]
    usable = (step > 1e-30) & (step < 1e30)
    return step, turn, jnp.where(usable, step, 1.0), jnp.where(usable, turn, 0.0)


def product2_kernel(
    ids, cols, dens, rows, tiles, factors, gram, gathered, scalars, image0, q0, q1,
    prev, sums, pieces, q2, zb, turned,
):
    _, turn, a, b = trial(scalars)
    q_two = (1.0 + b) * q1[...] - turn * q0[...] - a * gathered[...].reshape(q2.shape)
    q2[...] = q_two
    zb[...] = q_two.astype(BF16).reshape(zb.shape)
    share = total11(q_two * gram_product(q_two, gram[...]))
    at = own_rows(gathered.shape[1])
    v0, v1, q, p, w = image0[...], gathered[lax.axis_index("col")], q0[at, :], q1[at, :], q2[at, :]
    r = p - turn * q
    r2 = r - a * v1
    known = [dot11(r, r), dot11(r, r2), dot11(r2, r2), dot11(q, v0), dot11(q, v1), dot11(p, v0)]
    known += [dot11(p, v1), dot11(w, v0), dot11(w, v1)]
    share += RIDGE * dot11(w, w)
    for i, slab in enumerate((prev, q0, q1, q2)):
        pieces[i] = own_components(slab[...].astype(F32), turned.at[i])
    share += total11(data_curvature(ids, cols, dens, rows, factors, zb, tiles))
    sums[...] = jnp.broadcast_to(lanes(known + [share]), sums.shape)


def own_components(slab, turned):
    count = turned.shape[0] // lax.axis_size("col")
    turned[...] = slab.T
    return turned[pl.ds(pl.multiple_of(lax.axis_index("col") * count, count), count), :]


def finish_kernel(sums, scalars, pieces, out):
    totals = jnp.sum(sums[...], axis=0, keepdims=True)
    n11, n12, n22, c00, c01, c10, c11, c02, c12, c22 = (totals[:, i : i + 1] for i in range(10))
    step0, turn0, a, b = trial(scalars)
    step1 = n11 / (c11 + EPS)
    h = step1 / a
    rest = 1.0 - h
    norm2 = rest * rest * n11 + 2.0 * h * rest * n12 + h * h * n22
    turn1 = norm2 / (n11 + EPS)
    g0 = -rest * turn0
    g1 = rest + turn1 - h * b
    curvature = (
        g0 * g0 * c00 + g1 * g1 * c11 + h * h * c22
        + g0 * g1 * (c01 + c10) + 2.0 * (g0 * h * c02 + g1 * h * c12)
    )
    step2 = norm2 / (curvature + EPS)
    k0, k1, k2 = step0 + step2 * g0, step1 + step2 * g1, step2 * h
    out[...] = pieces[0] + k0 * pieces[1] + k1 * pieces[2] + k2 * pieces[3]


def gather_factors(col_factors, beside):
    nrow = lax.axis_size("row")
    blocks, height, width = col_factors.shape

    def from_z(x, shift):
        return lax.ppermute(x, "row", [(i, (i - 2 * shift) % nrow) for i in range(nrow)])

    own = col_factors.reshape(1, blocks * height, width)
    near = jnp.concatenate([from_z(own, 2), own, from_z(own, 6)])
    onward = jnp.where(lax.axis_index("row") % 2 == 0, near[:1], near[2:])
    onward = lax.ppermute(onward, "row", [(i, (i + (4 if i % 2 else -4)) % nrow) for i in range(nrow)])
    mine = jnp.concatenate([near, from_z(near[:2], 1), from_z(near[1:], 7), onward])
    shifts = (2, 0, 6, 3, 1, 7, 5, 4)
    mine, beside = lax.optimization_barrier((mine, beside))
    other = lax.ppermute(mine, "row", [(i, i ^ 1) for i in range(nrow)])
    whole = jax.ShapeDtypeStruct((blocks, nrow * height, width), BF16)
    assemble = call(functools.partial(assemble_kernel, shifts), whole, [VMEM, VMEM])
    return assemble(mine, other), beside


def local(tile_values, tile_rows, tile_cols, tile_counts, col_factors, prev_factors):
    tiles = tile_values[0, 0]
    count, size = tiles.shape[0], tiles.shape[1]
    width = col_factors.shape[2]
    height_all = prev_factors.shape[0]
    blocks = height_all // size
    ncol, nrow = lax.axis_size("col"), lax.axis_size("row")
    height = height_all // ncol

    slots = count + blocks
    order = call(
        plan_kernel,
        [
            jax.ShapeDtypeStruct((slots,), jnp.int32),
            jax.ShapeDtypeStruct((slots,), jnp.int32),
            jax.ShapeDtypeStruct((slots,), F32),
            jax.ShapeDtypeStruct((slots // 2,), jnp.int32),
        ],
        [pl.ANY] * 3,
        [SMEM((count,), jnp.int32)] * 3
        + [SMEM((blocks,), jnp.int32), pltpu.SemaphoreType.DMA((3,))],
        flops=BUSY,
        out_space=SMEM,
    )(tile_rows[0, 0], tile_cols[0, 0], tile_counts[0, 0])
    factors, order = gather_factors(col_factors, order)
    flat = factors.reshape(-1, width)
    gram = lax.dot_general(flat, flat, (((0,), (0,)), ((), ())), preferred_element_type=F32)

    def exchange(x):
        return lax.all_to_all(x, "col", 0, 0)

    slab = jax.ShapeDtypeStruct((height_all, width), F32)
    part = jax.ShapeDtypeStruct((blocks, size, width), F32)
    wide = jax.ShapeDtypeStruct((ncol, height, width), F32)
    zb = VMEM((blocks, size, width), BF16)
    common = (*order, tiles, factors, gram)
    spaces = [SMEM] * 4 + [VMEM] * 3

    def summed(sign, partial, p):
        parts = exchange(partial.reshape(ncol, height, width))
        shard = call(functools.partial(shard_kernel, sign), wide, [VMEM, VMEM], flops=BUSY)
        return exchange(shard(parts, p))

    partial = call(apply_first, part, spaces + [VMEM])(
        *common, prev_factors.reshape(blocks, size, width)
    )
    res0 = summed(-1.0, partial, prev_factors)
    partial, q0 = call(product0_kernel, [part, slab], spaces + [VMEM], [zb])(*common, res0)
    image0 = summed(1.0, partial, q0)
    sums, own0 = call(
        dots_kernel,
        [jax.ShapeDtypeStruct((nrow, width), F32), jax.ShapeDtypeStruct((height, width), F32)],
        [VMEM] * 2,
        flops=BUSY,
    )(image0, q0)
    sums = lax.all_to_all(sums, "row", 0, 0, tiled=True)
    small = jax.ShapeDtypeStruct((8, width), F32)
    partial, q1, scalars = call(
        product1_kernel, [part, slab, small], spaces + [VMEM] * 3, [zb]
    )(*common, image0, sums, q0)
    image1 = summed(1.0, partial, q1)
    piece = (width // ncol, height_all)
    sums, pieces = call(
        product2_kernel,
        [jax.ShapeDtypeStruct((nrow * ncol, width), F32), jax.ShapeDtypeStruct((4, *piece), F32)],
        spaces + [VMEM] * 6,
        [VMEM((height_all, width), F32), zb, VMEM((4, width, height_all), F32)],
    )(*common, image1, scalars, own0, q0, q1, prev_factors)
    sums = lax.all_to_all(sums, ("row", "col"), 0, 0, tiled=True)
    return call(finish_kernel, jax.ShapeDtypeStruct(piece, F32), [VMEM] * 3)(sums, scalars, pieces)


def solution(mesh):
    return jax.shard_map(
        local,
        mesh=mesh,
        in_specs=(
            P("row", "col", None, None, None),
            P("row", "col", None),
            P("row", "col", None),
            P("row", "col", None),
            P("col", "row", None),
            P("row", None),
        ),
        out_specs=P("col", "row"),
        check_vma=False,
    )
```

```python
import functools

import jax
import jax.numpy as jnp
from jax import lax
from jax.experimental import pallas as pl
from jax.experimental.pallas import tpu as pltpu
from jax.sharding import PartitionSpec as P

RIDGE = 0.1
EPS = 1e-12
UNROLL = 66
LAG = 6
TILE_AREA = 128 * 128
BUSY = 10_000_000_000
F32 = jnp.float32
BF16 = jnp.bfloat16
NT_DIMS = (((1,), (1,)), ((), ()))
VMEM = pltpu.VMEM
SMEM = pltpu.SMEM


def spec(space):
    return pl.BlockSpec(memory_space=space)


def call(kernel, out_shape, in_spaces, scratch=(), flops=None, out_space=VMEM):
    single = not isinstance(out_shape, (list, tuple))
    return pl.pallas_call(
        kernel,
        out_shape=out_shape,
        in_specs=[spec(s) for s in in_spaces],
        out_specs=spec(out_space) if single else [spec(out_space) for _ in out_shape],
        scratch_shapes=list(scratch),
        cost_estimate=flops
        and pl.CostEstimate(flops=flops, bytes_accessed=0, transcendentals=0),
        compiler_params=pltpu.CompilerParams(vmem_limit_bytes=16 * 1024 * 1024),
    )


def plan_kernel(table_in, ids, slot_cols, dens, pair_rows, table, fill, sem):
    copy = pltpu.make_async_copy(table_in, table, sem)
    copy.start()
    copy.wait()
    count, slots, blocks = table.shape[0] // 3, ids.shape[0], fill.shape[0]

    def tally(t, held):
        return tuple(n + (table[t] == r).astype(jnp.int32) for r, n in enumerate(held))

    held = lax.fori_loop(0, count, tally, (jnp.int32(0),) * blocks, unroll=16)
    at = jnp.int32(0)
    ends = []
    for r in range(blocks):
        fill[r] = at
        ends.append((held[r], at + held[r]))
        at = at + held[r] + held[r] % 2

    def put(s, tile, col, density, r):
        ids[s] = tile
        slot_cols[s] = col
        dens[s] = density
        pair_rows[s // 2] = r

    def place(t, carry):
        r = table[t]
        s = fill[r]
        fill[r] = s + 1
        put(s, t, table[count + t], table[2 * count + t].astype(F32) * (1.0 / TILE_AREA), r)
        return carry

    lax.fori_loop(0, count, place, 0, unroll=8)
    for r, (n, end) in enumerate(ends):

        @pl.when(n % 2 == 1)
        def _(r=r, end=end):
            put(end, 0, 0, 0.0, r)

    def rest(s, carry):
        put(s, 0, 0, 0.0, 0)
        return carry

    lax.fori_loop(at, slots, rest, 0)


def assemble_kernel(shifts, mine, other, out):
    me = lax.axis_index("row")
    first = me % 2 == 0
    blocks = out.shape[0]
    for i, shift in enumerate(shifts):
        a, b = mine[i].astype(F32), other[i].astype(F32)
        lo, hi = jnp.where(first, a, b), jnp.where(first, b, a)
        both = jnp.concatenate([x.reshape(blocks, -1, x.shape[1]) for x in (lo, hi)], axis=1)
        height = both.shape[1]
        at = (me // 2 + shift) % len(shifts) * height
        out[:, pl.ds(pl.multiple_of(at, height), height), :] = both.astype(BF16)


def unroll_of(pairs):
    return max(u for u in range(1, UNROLL + 1) if pairs % u == 0)


def over_pairs(rows, group, start):
    pairs = rows.shape[0]
    unroll = unroll_of(pairs)

    def step(g, carry):
        return group([g * unroll + u for u in range(unroll)], carry)

    return lax.fori_loop(0, pairs // unroll, step, start)


def pair_weights(flag, pair, ids, cols, dens, rows, tiles, factors, zb):
    slots = (2 * pair, 2 * pair + 1)
    both = jnp.concatenate([factors[cols[s]] for s in slots], axis=0)
    scores = lax.dot_general(zb[rows[pair]], both, NT_DIMS, preferred_element_type=F32)
    weights = []
    for i, s in enumerate(slots):
        score = scores[:, i * 128 : (i + 1) * 128]
        values = tiles[ids[s]].astype(F32)
        scaled = dens[s] * values
        w = scaled * values * score
        weights.append((score, scaled - w if flag else w))
    return both, weights


def data_product(flag, ids, cols, dens, rows, factors, zb, tiles, acc):
    def group(pairs, carry):
        held = []

        def add():
            row, w, both = held.pop(0)
            acc[row] += jnp.dot(w, both, preferred_element_type=F32)

        for pair in pairs:
            both, weights = pair_weights(flag, pair, ids, cols, dens, rows, tiles, factors, zb)
            w = jnp.concatenate([w.astype(BF16) for _, w in weights], axis=1)
            held.append((rows[pair], w, both))
            if len(held) > LAG:
                add()
        while held:
            add()
        return carry

    over_pairs(rows, group, 0)


def data_curvature(ids, cols, dens, rows, factors, zb, tiles):
    def group(pairs, total):
        for pair in pairs:
            _, weights = pair_weights(False, pair, ids, cols, dens, rows, tiles, factors, zb)
            for score, w in weights:
                total = total + jnp.sum((w * score).reshape(-1, *total.shape), axis=0)
        return total

    return over_pairs(rows, group, jnp.zeros((64, 128), F32))


def gram_product(p, gram):
    def halves(x, axis):
        hi = x.astype(BF16)
        return jnp.concatenate([hi, (x - hi.astype(F32)).astype(BF16)], axis=axis)

    row = halves(gram, 1)
    both = jnp.dot(halves(p, 1), jnp.concatenate([row, row], axis=0), preferred_element_type=F32)
    return both[:, : gram.shape[1]] + both[:, gram.shape[1] :]


def total11(x):
    return jnp.sum(jnp.sum(x, axis=0, keepdims=True), axis=1, keepdims=True)


def dot11(x, y):
    return total11(x * y)


def lanes(scalars):
    lane = lax.broadcasted_iota(jnp.int32, (1, 128), 1)
    row = jnp.zeros((1, 128), F32)
    for i, s in enumerate(scalars):
        row = jnp.where(lane == i, s, row)
    return row


def apply_first(ids, cols, dens, rows, tiles, factors, gram, prev, out):
    blocks, size, width = out.shape
    p = prev[...].astype(F32).reshape(blocks * size, width)
    out[...] = -gram_product(p, gram[...]).reshape(out.shape)
    data_product(True, ids, cols, dens, rows, factors, prev, tiles, out)


def apply_operator(ids, cols, dens, rows, factors, gram, p, zb, tiles, out):
    zb[...] = p.astype(BF16).reshape(zb.shape)
    out[...] = gram_product(p, gram[...]).reshape(out.shape)
    data_product(False, ids, cols, dens, rows, factors, zb, tiles, out)


def own_rows(height):
    return pl.ds(pl.multiple_of(lax.axis_index("col") * height, height), height)


def shard_of(parts, slab, sign):
    mine = slab[own_rows(parts.shape[1]), :].astype(F32)
    return jnp.sum(parts[...], axis=0) + sign * RIDGE * mine, mine


def shard_kernel(sign, parts, slab, out):
    shard, _ = shard_of(parts, slab, sign)
    out[...] = jnp.broadcast_to(shard[None], out.shape)


def dots_kernel(gathered, q0, sums, own):
    own[...] = gathered[lax.axis_index("col")]
    v, q = gathered[...].reshape(q0.shape), q0[...]
    top = jnp.max(jnp.max(jnp.abs(v), axis=0, keepdims=True), axis=1, keepdims=True)
    unit = v * jnp.where(top > 0.0, 1.0 / top, 0.0)
    row = lanes([dot11(q, v), dot11(q, q), dot11(unit, unit), top])
    sums[...] = jnp.broadcast_to(row, sums.shape)


def merge(rows):
    top = jnp.max(rows[:, 3:4], axis=0, keepdims=True)
    scale = rows[:, 3:4] * jnp.where(top > 0.0, 1.0 / top, 0.0)
    square = jnp.sum(rows[:, 2:3] * scale * scale, axis=0, keepdims=True)
    total = jnp.sum(rows, axis=0, keepdims=True)
    return total[:, 0:1], total[:, 1:2], square, top


def product0_kernel(
    ids, cols, dens, rows, tiles, factors, gram, gathered, out, q0, zb,
):
    q = gathered[...].reshape(q0.shape)
    q0[...] = q
    apply_operator(ids, cols, dens, rows, factors, gram, q, zb, tiles, out)


def product1_kernel(
    ids, cols, dens, rows, tiles, factors, gram, gathered, sums, q0, out, q1, scalars, zb,
):
    q, v = q0[...], gathered[...].reshape(q0.shape)
    curvature, norm, square, top = merge(sums[...])
    step = norm / (curvature + EPS)
    scaled = step * top
    following = jnp.maximum(norm - 2.0 * (step * curvature) + scaled * scaled * square, 0.0)
    turn = following / (norm + EPS)
    scalars[...] = jnp.broadcast_to(lanes([step, turn]), scalars.shape)
    q = (q - step * v) + turn * q
    q1[...] = q
    apply_operator(ids, cols, dens, rows, factors, gram, q, zb, tiles, out)


def trial(scalars):
    step, turn = scalars[:1, 0:1], scalars[:1, 1:2]
    usable = (step > 1e-30) & (step < 1e30)
    return step, turn, jnp.where(usable, step, 1.0), jnp.where(usable, turn, 0.0)


def product2_kernel(
    ids, cols, dens, rows, tiles, factors, gram, gathered, scalars, image0, q0, q1,
    prev, sums, pieces, q2, zb, turned,
):
    _, turn, a, b = trial(scalars)
    q_two = (1.0 + b) * q1[...] - turn * q0[...] - a * gathered[...].reshape(q2.shape)
    q2[...] = q_two
    zb[...] = q_two.astype(BF16).reshape(zb.shape)
    share = total11(q_two * gram_product(q_two, gram[...]))
    at = own_rows(gathered.shape[1])
    v0, v1, q, p, w = image0[...], gathered[lax.axis_index("col")], q0[at, :], q1[at, :], q2[at, :]
    r = p - turn * q
    r2 = r - a * v1
    known = [dot11(r, r), dot11(r, r2), dot11(r2, r2), dot11(q, v0), dot11(q, v1), dot11(p, v0)]
    known += [dot11(p, v1), dot11(w, v0), dot11(w, v1)]
    share += RIDGE * dot11(w, w)
    for i, slab in enumerate((prev, q0, q1, q2)):
        pieces[i] = own_components(slab[...].astype(F32), turned.at[i])
    share += total11(data_curvature(ids, cols, dens, rows, factors, zb, tiles))
    sums[...] = jnp.broadcast_to(lanes(known + [share]), sums.shape)


def own_components(slab, turned):
    count = turned.shape[0] // lax.axis_size("col")
    turned[...] = slab.T
    return turned[pl.ds(pl.multiple_of(lax.axis_index("col") * count, count), count), :]


def finish_kernel(sums, scalars, pieces, out):
    totals = jnp.sum(sums[...], axis=0, keepdims=True)
    n11, n12, n22, c00, c01, c10, c11, c02, c12, c22 = (totals[:, i : i + 1] for i in range(10))
    step0, turn0, a, b = trial(scalars)
    step1 = n11 / (c11 + EPS)
    h = step1 / a
    rest = 1.0 - h
    norm2 = rest * rest * n11 + 2.0 * h * rest * n12 + h * h * n22
    turn1 = norm2 / (n11 + EPS)
    g0 = -rest * turn0
    g1 = rest + turn1 - h * b
    curvature = (
        g0 * g0 * c00 + g1 * g1 * c11 + h * h * c22
        + g0 * g1 * (c01 + c10) + 2.0 * (g0 * h * c02 + g1 * h * c12)
    )
    step2 = norm2 / (curvature + EPS)
    k0, k1, k2 = step0 + step2 * g0, step1 + step2 * g1, step2 * h
    out[...] = pieces[0] + k0 * pieces[1] + k1 * pieces[2] + k2 * pieces[3]


def gather_factors(col_factors, beside):
    nrow = lax.axis_size("row")
    blocks, height, width = col_factors.shape

    def from_z(x, shift):
        return lax.ppermute(x, "row", [(i, (i - 2 * shift) % nrow) for i in range(nrow)])

    own = col_factors.reshape(1, blocks * height, width)
    near = jnp.concatenate([from_z(own, 2), own, from_z(own, 6)])
    onward = jnp.where(lax.axis_index("row") % 2 == 0, near[:1], near[2:])
    onward = lax.ppermute(onward, "row", [(i, (i + (4 if i % 2 else -4)) % nrow) for i in range(nrow)])
    mine = jnp.concatenate([near, from_z(near[:2], 1), from_z(near[1:], 7), onward])
    shifts = (2, 0, 6, 3, 1, 7, 5, 4)
    mine, beside = lax.optimization_barrier((mine, beside))
    other = lax.ppermute(mine, "row", [(i, i ^ 1) for i in range(nrow)])
    whole = jax.ShapeDtypeStruct((blocks, nrow * height, width), BF16)
    assemble = call(functools.partial(assemble_kernel, shifts), whole, [VMEM, VMEM])
    return assemble(mine, other), beside


def local(tile_values, tile_rows, tile_cols, tile_counts, col_factors, prev_factors):
    tiles = tile_values[0, 0]
    count, size = tiles.shape[0], tiles.shape[1]
    width = col_factors.shape[2]
    height_all = prev_factors.shape[0]
    blocks = height_all // size
    ncol, nrow = lax.axis_size("col"), lax.axis_size("row")
    height = height_all // ncol

    slots = count + blocks
    order = call(
        plan_kernel,
        [
            jax.ShapeDtypeStruct((slots,), jnp.int32),
            jax.ShapeDtypeStruct((slots,), jnp.int32),
            jax.ShapeDtypeStruct((slots,), F32),
            jax.ShapeDtypeStruct((slots // 2,), jnp.int32),
        ],
        [pl.ANY],
        [SMEM((3 * count,), jnp.int32), SMEM((blocks,), jnp.int32), pltpu.SemaphoreType.DMA],
        flops=BUSY,
        out_space=SMEM,
    )(jnp.concatenate([tile_rows[0, 0], tile_cols[0, 0], tile_counts[0, 0]]))
    factors, order = gather_factors(col_factors, order)
    flat = factors.reshape(-1, width)
    gram = lax.dot_general(flat, flat, (((0,), (0,)), ((), ())), preferred_element_type=F32)

    def exchange(x):
        return lax.all_to_all(x, "col", 0, 0)

    slab = jax.ShapeDtypeStruct((height_all, width), F32)
    part = jax.ShapeDtypeStruct((blocks, size, width), F32)
    wide = jax.ShapeDtypeStruct((ncol, height, width), F32)
    zb = VMEM((blocks, size, width), BF16)
    common = (*order, tiles, factors, gram)
    spaces = [SMEM] * 4 + [VMEM] * 3

    def summed(sign, partial, p):
        parts = exchange(partial.reshape(ncol, height, width))
        shard = call(functools.partial(shard_kernel, sign), wide, [VMEM, VMEM], flops=BUSY)
        return exchange(shard(parts, p))

    partial = call(apply_first, part, spaces + [VMEM])(
        *common, prev_factors.reshape(blocks, size, width)
    )
    res0 = summed(-1.0, partial, prev_factors)
    partial, q0 = call(product0_kernel, [part, slab], spaces + [VMEM], [zb])(*common, res0)
    image0 = summed(1.0, partial, q0)
    sums, own0 = call(
        dots_kernel,
        [jax.ShapeDtypeStruct((nrow, width), F32), jax.ShapeDtypeStruct((height, width), F32)],
        [VMEM] * 2,
        flops=BUSY,
    )(image0, q0)
    sums = lax.all_to_all(sums, "row", 0, 0, tiled=True)
    small = jax.ShapeDtypeStruct((8, width), F32)
    partial, q1, scalars = call(
        product1_kernel, [part, slab, small], spaces + [VMEM] * 3, [zb]
    )(*common, image0, sums, q0)
    image1 = summed(1.0, partial, q1)
    piece = (width // ncol, height_all)
    sums, pieces = call(
        product2_kernel,
        [jax.ShapeDtypeStruct((nrow * ncol, width), F32), jax.ShapeDtypeStruct((4, *piece), F32)],
        spaces + [VMEM] * 6,
        [VMEM((height_all, width), F32), zb, VMEM((4, width, height_all), F32)],
    )(*common, image1, scalars, own0, q0, q1, prev_factors)
    sums = lax.all_to_all(sums, ("row", "col"), 0, 0, tiled=True)
    return call(finish_kernel, jax.ShapeDtypeStruct(piece, F32), [VMEM] * 3)(sums, scalars, pieces)


def solution(mesh):
    return jax.shard_map(
        local,
        mesh=mesh,
        in_specs=(
            P("row", "col", None, None, None),
            P("row", "col", None),
            P("row", "col", None),
            P("row", "col", None),
            P("col", "row", None),
            P("row", None),
        ),
        out_specs=P("col", "row"),
        check_vma=False,
    )
```

```python
import functools

import jax
import jax.numpy as jnp
from jax import lax
from jax.experimental import pallas as pl
from jax.experimental.pallas import tpu as pltpu
from jax.sharding import PartitionSpec as P

RIDGE = 0.1
EPS = 1e-12
UNROLL = 66
LAG = 6
TILE_AREA = 128 * 128
BUSY = 10_000_000_000
F32 = jnp.float32
BF16 = jnp.bfloat16
NT_DIMS = (((1,), (1,)), ((), ()))
VMEM = pltpu.VMEM
SMEM = pltpu.SMEM


def spec(space):
    return pl.BlockSpec(memory_space=space)


def call(kernel, out_shape, in_spaces, scratch=(), flops=None, out_space=VMEM):
    single = not isinstance(out_shape, (list, tuple))
    return pl.pallas_call(
        kernel,
        out_shape=out_shape,
        in_specs=[spec(s) for s in in_spaces],
        out_specs=spec(out_space) if single else [spec(out_space) for _ in out_shape],
        scratch_shapes=list(scratch),
        cost_estimate=flops
        and pl.CostEstimate(flops=flops, bytes_accessed=0, transcendentals=0),
        compiler_params=pltpu.CompilerParams(vmem_limit_bytes=16 * 1024 * 1024),
    )


def plan_kernel(table_in, ids, slot_cols, dens, pair_rows, table, fill, sem):
    copy = pltpu.make_async_copy(table_in, table, sem)
    copy.start()
    copy.wait()
    count, slots, blocks = table.shape[0] // 3, ids.shape[0], fill.shape[0]

    def tally(t, held):
        return tuple(n + (table[t] == r).astype(jnp.int32) for r, n in enumerate(held))

    held = lax.fori_loop(0, count, tally, (jnp.int32(0),) * blocks, unroll=16)
    at = jnp.int32(0)
    ends = []
    for r in range(blocks):
        fill[r] = at
        ends.append((held[r], at + held[r]))
        at = at + held[r] + held[r] % 2

    def put(s, tile, col, density, r):
        ids[s] = tile
        slot_cols[s] = col
        dens[s] = density
        pair_rows[s // 2] = r

    def place(t, carry):
        r = table[t]
        s = fill[r]
        fill[r] = s + 1
        put(s, t, table[count + t], table[2 * count + t].astype(F32) * (1.0 / TILE_AREA), r)
        return carry

    lax.fori_loop(0, count, place, 0, unroll=8)
    for r, (n, end) in enumerate(ends):

        @pl.when(n % 2 == 1)
        def _(r=r, end=end):
            put(end, 0, 0, 0.0, r)

    def rest(s, carry):
        put(s, 0, 0, 0.0, 0)
        return carry

    lax.fori_loop(at, slots, rest, 0)


def assemble_kernel(shifts, near, near_other, rest, rest_other, out):
    mine = [x.at[i] for x in (near, rest) for i in range(x.shape[0])]
    other = [x.at[i] for x in (near_other, rest_other) for i in range(x.shape[0])]
    me = lax.axis_index("row")
    first = me % 2 == 0
    blocks = out.shape[0]
    for i, shift in enumerate(shifts):
        a, b = mine[i][...].astype(F32), other[i][...].astype(F32)
        lo, hi = jnp.where(first, a, b), jnp.where(first, b, a)
        both = jnp.concatenate([x.reshape(blocks, -1, x.shape[1]) for x in (lo, hi)], axis=1)
        height = both.shape[1]
        at = (me // 2 + shift) % len(shifts) * height
        out[:, pl.ds(pl.multiple_of(at, height), height), :] = both.astype(BF16)


def unroll_of(pairs):
    return max(u for u in range(1, UNROLL + 1) if pairs % u == 0)


def over_pairs(rows, group, start):
    pairs = rows.shape[0]
    unroll = unroll_of(pairs)

    def step(g, carry):
        return group([g * unroll + u for u in range(unroll)], carry)

    return lax.fori_loop(0, pairs // unroll, step, start)


def pair_weights(flag, pair, ids, cols, dens, rows, tiles, factors, zb):
    slots = (2 * pair, 2 * pair + 1)
    both = jnp.concatenate([factors[cols[s]] for s in slots], axis=0)
    scores = lax.dot_general(zb[rows[pair]], both, NT_DIMS, preferred_element_type=F32)
    weights = []
    for i, s in enumerate(slots):
        score = scores[:, i * 128 : (i + 1) * 128]
        values = tiles[ids[s]].astype(F32)
        scaled = dens[s] * values
        w = scaled * values * score
        weights.append((score, scaled - w if flag else w))
    return both, weights


def data_product(flag, ids, cols, dens, rows, factors, zb, tiles, acc):
    def group(pairs, carry):
        held = []

        def add():
            row, w, both = held.pop(0)
            acc[row] += jnp.dot(w, both, preferred_element_type=F32)

        for pair in pairs:
            both, weights = pair_weights(flag, pair, ids, cols, dens, rows, tiles, factors, zb)
            w = jnp.concatenate([w.astype(BF16) for _, w in weights], axis=1)
            held.append((rows[pair], w, both))
            if len(held) > LAG:
                add()
        while held:
            add()
        return carry

    over_pairs(rows, group, 0)


def data_curvature(ids, cols, dens, rows, factors, zb, tiles):
    def group(pairs, total):
        for pair in pairs:
            _, weights = pair_weights(False, pair, ids, cols, dens, rows, tiles, factors, zb)
            for score, w in weights:
                total = total + jnp.sum((w * score).reshape(-1, *total.shape), axis=0)
        return total

    return over_pairs(rows, group, jnp.zeros((64, 128), F32))


def gram_product(p, gram):
    def halves(x, axis):
        hi = x.astype(BF16)
        return jnp.concatenate([hi, (x - hi.astype(F32)).astype(BF16)], axis=axis)

    row = halves(gram, 1)
    both = jnp.dot(halves(p, 1), jnp.concatenate([row, row], axis=0), preferred_element_type=F32)
    return both[:, : gram.shape[1]] + both[:, gram.shape[1] :]


def total11(x):
    return jnp.sum(jnp.sum(x, axis=0, keepdims=True), axis=1, keepdims=True)


def dot11(x, y):
    return total11(x * y)


def lanes(scalars):
    lane = lax.broadcasted_iota(jnp.int32, (1, 128), 1)
    row = jnp.zeros((1, 128), F32)
    for i, s in enumerate(scalars):
        row = jnp.where(lane == i, s, row)
    return row


def apply_first(ids, cols, dens, rows, tiles, factors, gram, prev, out):
    blocks, size, width = out.shape
    p = prev[...].astype(F32).reshape(blocks * size, width)
    out[...] = -gram_product(p, gram[...]).reshape(out.shape)
    data_product(True, ids, cols, dens, rows, factors, prev, tiles, out)


def apply_operator(ids, cols, dens, rows, factors, gram, p, zb, tiles, out):
    zb[...] = p.astype(BF16).reshape(zb.shape)
    out[...] = gram_product(p, gram[...]).reshape(out.shape)
    data_product(False, ids, cols, dens, rows, factors, zb, tiles, out)


def own_rows(height):
    return pl.ds(pl.multiple_of(lax.axis_index("col") * height, height), height)


def shard_of(parts, slab, sign):
    mine = slab[own_rows(parts.shape[1]), :].astype(F32)
    return jnp.sum(parts[...], axis=0) + sign * RIDGE * mine, mine


def shard_kernel(sign, parts, slab, out):
    shard, _ = shard_of(parts, slab, sign)
    out[...] = jnp.broadcast_to(shard[None], out.shape)


def dots_kernel(gathered, q0, sums, own):
    own[...] = gathered[lax.axis_index("col")]
    v, q = gathered[...].reshape(q0.shape), q0[...]
    top = jnp.max(jnp.max(jnp.abs(v), axis=0, keepdims=True), axis=1, keepdims=True)
    unit = v * jnp.where(top > 0.0, 1.0 / top, 0.0)
    row = lanes([dot11(q, v), dot11(q, q), dot11(unit, unit), top])
    sums[...] = jnp.broadcast_to(row, sums.shape)


def merge(rows):
    top = jnp.max(rows[:, 3:4], axis=0, keepdims=True)
    scale = rows[:, 3:4] * jnp.where(top > 0.0, 1.0 / top, 0.0)
    square = jnp.sum(rows[:, 2:3] * scale * scale, axis=0, keepdims=True)
    total = jnp.sum(rows, axis=0, keepdims=True)
    return total[:, 0:1], total[:, 1:2], square, top


def product0_kernel(
    ids, cols, dens, rows, tiles, factors, gram, gathered, out, q0, zb,
):
    q = gathered[...].reshape(q0.shape)
    q0[...] = q
    apply_operator(ids, cols, dens, rows, factors, gram, q, zb, tiles, out)


def product1_kernel(
    ids, cols, dens, rows, tiles, factors, gram, gathered, sums, q0, out, q1, scalars, zb,
):
    q, v = q0[...], gathered[...].reshape(q0.shape)
    curvature, norm, square, top = merge(sums[...])
    step = norm / (curvature + EPS)
    scaled = step * top
    following = jnp.maximum(norm - 2.0 * (step * curvature) + scaled * scaled * square, 0.0)
    turn = following / (norm + EPS)
    scalars[...] = jnp.broadcast_to(lanes([step, turn]), scalars.shape)
    q = (q - step * v) + turn * q
    q1[...] = q
    apply_operator(ids, cols, dens, rows, factors, gram, q, zb, tiles, out)


def trial(scalars):
    step, turn = scalars[:1, 0:1], scalars[:1, 1:2]
    usable = (step > 1e-30) & (step < 1e30)
    return step, turn, jnp.where(usable, step, 1.0), jnp.where(usable, turn, 0.0)


def product2_kernel(
    ids, cols, dens, rows, tiles, factors, gram, gathered, scalars, image0, q0, q1,
    prev, sums, pieces, q2, zb, turned,
):
    _, turn, a, b = trial(scalars)
    q_two = (1.0 + b) * q1[...] - turn * q0[...] - a * gathered[...].reshape(q2.shape)
    q2[...] = q_two
    zb[...] = q_two.astype(BF16).reshape(zb.shape)
    share = total11(q_two * gram_product(q_two, gram[...]))
    at = own_rows(gathered.shape[1])
    v0, v1, q, p, w = image0[...], gathered[lax.axis_index("col")], q0[at, :], q1[at, :], q2[at, :]
    r = p - turn * q
    r2 = r - a * v1
    known = [dot11(r, r), dot11(r, r2), dot11(r2, r2), dot11(q, v0), dot11(q, v1), dot11(p, v0)]
    known += [dot11(p, v1), dot11(w, v0), dot11(w, v1)]
    share += RIDGE * dot11(w, w)
    for i, slab in enumerate((prev, q0, q1, q2)):
        pieces[i] = own_components(slab[...].astype(F32), turned.at[i])
    share += total11(data_curvature(ids, cols, dens, rows, factors, zb, tiles))
    sums[...] = jnp.broadcast_to(lanes(known + [share]), sums.shape)


def own_components(slab, turned):
    count = turned.shape[0] // lax.axis_size("col")
    turned[...] = slab.T
    return turned[pl.ds(pl.multiple_of(lax.axis_index("col") * count, count), count), :]


def finish_kernel(sums, scalars, pieces, out):
    totals = jnp.sum(sums[...], axis=0, keepdims=True)
    n11, n12, n22, c00, c01, c10, c11, c02, c12, c22 = (totals[:, i : i + 1] for i in range(10))
    step0, turn0, a, b = trial(scalars)
    step1 = n11 / (c11 + EPS)
    h = step1 / a
    rest = 1.0 - h
    norm2 = rest * rest * n11 + 2.0 * h * rest * n12 + h * h * n22
    turn1 = norm2 / (n11 + EPS)
    g0 = -rest * turn0
    g1 = rest + turn1 - h * b
    curvature = (
        g0 * g0 * c00 + g1 * g1 * c11 + h * h * c22
        + g0 * g1 * (c01 + c10) + 2.0 * (g0 * h * c02 + g1 * h * c12)
    )
    step2 = norm2 / (curvature + EPS)
    k0, k1, k2 = step0 + step2 * g0, step1 + step2 * g1, step2 * h
    out[...] = pieces[0] + k0 * pieces[1] + k1 * pieces[2] + k2 * pieces[3]


def gather_factors(col_factors, beside):
    nrow = lax.axis_size("row")
    blocks, height, width = col_factors.shape

    def from_z(x, shift):
        return lax.ppermute(x, "row", [(i, (i - 2 * shift) % nrow) for i in range(nrow)])

    own = col_factors.reshape(1, blocks * height, width)
    near = jnp.concatenate([from_z(own, 2), own, from_z(own, 6)])
    onward = jnp.where(lax.axis_index("row") % 2 == 0, near[:1], near[2:])
    onward = lax.ppermute(onward, "row", [(i, (i + (4 if i % 2 else -4)) % nrow) for i in range(nrow)])
    rest = jnp.concatenate([from_z(near[:2], 1), from_z(near[1:], 7), onward])
    shifts = (2, 0, 6, 3, 1, 7, 5, 4)
    rest, beside = lax.optimization_barrier((rest, beside))

    def swap(x):
        return lax.ppermute(x, "row", [(i, i ^ 1) for i in range(nrow)])

    whole = jax.ShapeDtypeStruct((blocks, nrow * height, width), BF16)
    assemble = call(functools.partial(assemble_kernel, shifts), whole, [VMEM] * 4)
    return assemble(near, swap(near), rest, swap(rest)), beside


def local(tile_values, tile_rows, tile_cols, tile_counts, col_factors, prev_factors):
    tiles = tile_values[0, 0]
    count, size = tiles.shape[0], tiles.shape[1]
    width = col_factors.shape[2]
    height_all = prev_factors.shape[0]
    blocks = height_all // size
    ncol, nrow = lax.axis_size("col"), lax.axis_size("row")
    height = height_all // ncol

    slots = count + blocks
    order = call(
        plan_kernel,
        [
            jax.ShapeDtypeStruct((slots,), jnp.int32),
            jax.ShapeDtypeStruct((slots,), jnp.int32),
            jax.ShapeDtypeStruct((slots,), F32),
            jax.ShapeDtypeStruct((slots // 2,), jnp.int32),
        ],
        [pl.ANY],
        [SMEM((3 * count,), jnp.int32), SMEM((blocks,), jnp.int32), pltpu.SemaphoreType.DMA],
        flops=BUSY,
        out_space=SMEM,
    )(jnp.concatenate([tile_rows[0, 0], tile_cols[0, 0], tile_counts[0, 0]]))
    factors, order = gather_factors(col_factors, order)
    flat = factors.reshape(-1, width)
    gram = lax.dot_general(flat, flat, (((0,), (0,)), ((), ())), preferred_element_type=F32)

    def exchange(x):
        return lax.all_to_all(x, "col", 0, 0)

    slab = jax.ShapeDtypeStruct((height_all, width), F32)
    part = jax.ShapeDtypeStruct((blocks, size, width), F32)
    wide = jax.ShapeDtypeStruct((ncol, height, width), F32)
    zb = VMEM((blocks, size, width), BF16)
    common = (*order, tiles, factors, gram)
    spaces = [SMEM] * 4 + [VMEM] * 3

    def summed(sign, partial, p):
        parts = exchange(partial.reshape(ncol, height, width))
        shard = call(functools.partial(shard_kernel, sign), wide, [VMEM, VMEM], flops=BUSY)
        return exchange(shard(parts, p))

    partial = call(apply_first, part, spaces + [VMEM])(
        *common, prev_factors.reshape(blocks, size, width)
    )
    res0 = summed(-1.0, partial, prev_factors)
    partial, q0 = call(product0_kernel, [part, slab], spaces + [VMEM], [zb])(*common, res0)
    image0 = summed(1.0, partial, q0)
    sums, own0 = call(
        dots_kernel,
        [jax.ShapeDtypeStruct((nrow, width), F32), jax.ShapeDtypeStruct((height, width), F32)],
        [VMEM] * 2,
        flops=BUSY,
    )(image0, q0)
    sums = lax.all_to_all(sums, "row", 0, 0, tiled=True)
    small = jax.ShapeDtypeStruct((8, width), F32)
    partial, q1, scalars = call(
        product1_kernel, [part, slab, small], spaces + [VMEM] * 3, [zb]
    )(*common, image0, sums, q0)
    image1 = summed(1.0, partial, q1)
    piece = (width // ncol, height_all)
    sums, pieces = call(
        product2_kernel,
        [jax.ShapeDtypeStruct((nrow * ncol, width), F32), jax.ShapeDtypeStruct((4, *piece), F32)],
        spaces + [VMEM] * 6,
        [VMEM((height_all, width), F32), zb, VMEM((4, width, height_all), F32)],
    )(*common, image1, scalars, own0, q0, q1, prev_factors)
    sums = lax.all_to_all(sums, ("row", "col"), 0, 0, tiled=True)
    return call(finish_kernel, jax.ShapeDtypeStruct(piece, F32), [VMEM] * 3)(sums, scalars, pieces)


def solution(mesh):
    return jax.shard_map(
        local,
        mesh=mesh,
        in_specs=(
            P("row", "col", None, None, None),
            P("row", "col", None),
            P("row", "col", None),
            P("row", "col", None),
            P("col", "row", None),
            P("row", None),
        ),
        out_specs=P("col", "row"),
        check_vma=False,
    )
```

```python
import functools

import jax
import jax.numpy as jnp
from jax import lax
from jax.experimental import pallas as pl
from jax.experimental.pallas import tpu as pltpu
from jax.sharding import PartitionSpec as P

RIDGE = 0.1
EPS = 1e-12
UNROLL = 66
LAG = 6
TILE_AREA = 128 * 128
BUSY = 10_000_000_000
F32 = jnp.float32
BF16 = jnp.bfloat16
NT_DIMS = (((1,), (1,)), ((), ()))
VMEM = pltpu.VMEM
SMEM = pltpu.SMEM


def spec(space):
    return pl.BlockSpec(memory_space=space)


def call(kernel, out_shape, in_spaces, scratch=(), flops=None, out_space=VMEM):
    single = not isinstance(out_shape, (list, tuple))
    return pl.pallas_call(
        kernel,
        out_shape=out_shape,
        in_specs=[spec(s) for s in in_spaces],
        out_specs=spec(out_space) if single else [spec(out_space) for _ in out_shape],
        scratch_shapes=list(scratch),
        cost_estimate=flops
        and pl.CostEstimate(flops=flops, bytes_accessed=0, transcendentals=0),
        compiler_params=pltpu.CompilerParams(vmem_limit_bytes=16 * 1024 * 1024),
    )


def plan_kernel(table_in, ids, slot_cols, dens, pair_rows, table, fill, sem):
    copy = pltpu.make_async_copy(table_in, table, sem)
    copy.start()
    copy.wait()
    count, slots, blocks = table.shape[0] // 3, ids.shape[0], fill.shape[0]

    def tally(t, held):
        return tuple(n + (table[t] == r).astype(jnp.int32) for r, n in enumerate(held))

    held = lax.fori_loop(0, count, tally, (jnp.int32(0),) * blocks, unroll=16)
    at = jnp.int32(0)
    ends = []
    for r in range(blocks):
        fill[r] = at
        ends.append((held[r], at + held[r]))
        at = at + held[r] + held[r] % 2

    def put(s, tile, col, density, r):
        ids[s] = tile
        slot_cols[s] = col
        dens[s] = density
        pair_rows[s // 2] = r

    def place(t, carry):
        r = table[t]
        s = fill[r]
        fill[r] = s + 1
        put(s, t, table[count + t], table[2 * count + t].astype(F32) * (1.0 / TILE_AREA), r)
        return carry

    lax.fori_loop(0, count, place, 0, unroll=8)
    for r, (n, end) in enumerate(ends):

        @pl.when(n % 2 == 1)
        def _(r=r, end=end):
            put(end, 0, 0, 0.0, r)

    def rest(s, carry):
        put(s, 0, 0, 0.0, 0)
        return carry

    lax.fori_loop(at, slots, rest, 0)


def assemble_kernel(shifts, mine, other, out):
    me = lax.axis_index("row")
    first = me % 2 == 0
    blocks = out.shape[0]
    for i, shift in enumerate(shifts):
        a, b = mine[i].astype(F32), other[i].astype(F32)
        lo, hi = jnp.where(first, a, b), jnp.where(first, b, a)
        both = jnp.concatenate([x.reshape(blocks, -1, x.shape[1]) for x in (lo, hi)], axis=1)
        height = both.shape[1]
        at = (me // 2 + shift) % len(shifts) * height
        out[:, pl.ds(pl.multiple_of(at, height), height), :] = both.astype(BF16)


def unroll_of(pairs):
    return max(u for u in range(1, UNROLL + 1) if pairs % u == 0)


def over_pairs(rows, group, start):
    pairs = rows.shape[0]
    unroll = unroll_of(pairs)

    def step(g, carry):
        return group([g * unroll + u for u in range(unroll)], carry)

    return lax.fori_loop(0, pairs // unroll, step, start)


def pair_weights(flag, pair, ids, cols, dens, rows, tiles, factors, zb):
    slots = (2 * pair, 2 * pair + 1)
    both = jnp.concatenate([factors[cols[s]] for s in slots], axis=0)
    scores = lax.dot_general(zb[rows[pair]], both, NT_DIMS, preferred_element_type=F32)
    weights = []
    for i, s in enumerate(slots):
        score = scores[:, i * 128 : (i + 1) * 128]
        values = tiles[ids[s]].astype(F32)
        scaled = dens[s] * values
        w = scaled * values * score
        weights.append((score, scaled - w if flag else w))
    return both, weights


def data_product(flag, ids, cols, dens, rows, factors, zb, tiles, acc):
    def group(pairs, carry):
        held = []

        def add():
            row, w, both = held.pop(0)
            acc[row] += jnp.dot(w, both, preferred_element_type=F32)

        for pair in pairs:
            both, weights = pair_weights(flag, pair, ids, cols, dens, rows, tiles, factors, zb)
            w = jnp.concatenate([w.astype(BF16) for _, w in weights], axis=1)
            held.append((rows[pair], w, both))
            if len(held) > LAG:
                add()
        while held:
            add()
        return carry

    over_pairs(rows, group, 0)


def data_curvature(ids, cols, dens, rows, factors, zb, tiles):
    def group(pairs, total):
        for pair in pairs:
            _, weights = pair_weights(False, pair, ids, cols, dens, rows, tiles, factors, zb)
            for score, w in weights:
                total = total + jnp.sum((w * score).reshape(-1, *total.shape), axis=0)
        return total

    return over_pairs(rows, group, jnp.zeros((64, 128), F32))


def gram_product(p, gram):
    def halves(x, axis):
        hi = x.astype(BF16)
        return jnp.concatenate([hi, (x - hi.astype(F32)).astype(BF16)], axis=axis)

    row = halves(gram, 1)
    both = jnp.dot(halves(p, 1), jnp.concatenate([row, row], axis=0), preferred_element_type=F32)
    return both[:, : gram.shape[1]] + both[:, gram.shape[1] :]


def total11(x):
    return jnp.sum(jnp.sum(x, axis=0, keepdims=True), axis=1, keepdims=True)


def dot11(x, y):
    return total11(x * y)


def lanes(scalars):
    lane = lax.broadcasted_iota(jnp.int32, (1, 128), 1)
    row = jnp.zeros((1, 128), F32)
    for i, s in enumerate(scalars):
        row = jnp.where(lane == i, s, row)
    return row


def apply_first(ids, cols, dens, rows, tiles, factors, gram, prev, out):
    blocks, size, width = out.shape
    p = prev[...].astype(F32).reshape(blocks * size, width)
    out[...] = -gram_product(p, gram[...]).reshape(out.shape)
    data_product(True, ids, cols, dens, rows, factors, prev, tiles, out)


def apply_operator(ids, cols, dens, rows, factors, gram, p, zb, tiles, out):
    zb[...] = p.astype(BF16).reshape(zb.shape)
    out[...] = gram_product(p, gram[...]).reshape(out.shape)
    data_product(False, ids, cols, dens, rows, factors, zb, tiles, out)


def own_rows(height):
    return pl.ds(pl.multiple_of(lax.axis_index("col") * height, height), height)


def shard_of(parts, slab, sign):
    mine = slab[own_rows(parts.shape[1]), :].astype(F32)
    return jnp.sum(parts[...], axis=0) + sign * RIDGE * mine, mine


def shard_kernel(sign, parts, slab, out):
    shard, _ = shard_of(parts, slab, sign)
    out[...] = jnp.broadcast_to(shard[None], out.shape)


def dots_kernel(gathered, q0, sums, own):
    own[...] = gathered[lax.axis_index("col")]
    v, q = gathered[...].reshape(q0.shape), q0[...]
    top = jnp.max(jnp.max(jnp.abs(v), axis=0, keepdims=True), axis=1, keepdims=True)
    unit = v * jnp.where(top > 0.0, 1.0 / top, 0.0)
    row = lanes([dot11(q, v), dot11(q, q), dot11(unit, unit), top])
    sums[...] = jnp.broadcast_to(row, sums.shape)


def merge(rows):
    top = jnp.max(rows[:, 3:4], axis=0, keepdims=True)
    scale = rows[:, 3:4] * jnp.where(top > 0.0, 1.0 / top, 0.0)
    square = jnp.sum(rows[:, 2:3] * scale * scale, axis=0, keepdims=True)
    total = jnp.sum(rows, axis=0, keepdims=True)
    return total[:, 0:1], total[:, 1:2], square, top


def product0_kernel(
    ids, cols, dens, rows, tiles, factors, gram, gathered, out, q0, zb,
):
    q = gathered[...].reshape(q0.shape)
    q0[...] = q
    apply_operator(ids, cols, dens, rows, factors, gram, q, zb, tiles, out)


def product1_kernel(
    ids, cols, dens, rows, tiles, factors, gram, gathered, sums, q0, out, q1, scalars, zb,
):
    q, v = q0[...], gathered[...].reshape(q0.shape)
    curvature, norm, square, top = merge(sums[...])
    step = norm / (curvature + EPS)
    scaled = step * top
    following = jnp.maximum(norm - 2.0 * (step * curvature) + scaled * scaled * square, 0.0)
    turn = following / (norm + EPS)
    scalars[...] = jnp.broadcast_to(lanes([step, turn]), scalars.shape)
    q = (q - step * v) + turn * q
    q1[...] = q
    apply_operator(ids, cols, dens, rows, factors, gram, q, zb, tiles, out)


def trial(scalars):
    step, turn = scalars[:1, 0:1], scalars[:1, 1:2]
    usable = (step > 1e-30) & (step < 1e30)
    return step, turn, jnp.where(usable, step, 1.0), jnp.where(usable, turn, 0.0)


def product2_kernel(
    ids, cols, dens, rows, tiles, factors, gram, gathered, scalars, image0, q0, q1,
    prev, sums, pieces, q2, zb, turned,
):
    _, turn, a, b = trial(scalars)
    q_two = (1.0 + b) * q1[...] - turn * q0[...] - a * gathered[...].reshape(q2.shape)
    q2[...] = q_two
    zb[...] = q_two.astype(BF16).reshape(zb.shape)
    share = total11(q_two * gram_product(q_two, gram[...]))
    at = own_rows(gathered.shape[1])
    v0, v1, q, p, w = image0[...], gathered[lax.axis_index("col")], q0[at, :], q1[at, :], q2[at, :]
    r = p - turn * q
    r2 = r - a * v1
    known = [dot11(r, r), dot11(r, r2), dot11(r2, r2), dot11(q, v0), dot11(q, v1), dot11(p, v0)]
    known += [dot11(p, v1), dot11(w, v0), dot11(w, v1)]
    share += RIDGE * dot11(w, w)
    for i, slab in enumerate((prev, q0, q1, q2)):
        pieces[i] = own_components(slab[...].astype(F32), turned.at[i])
    share += total11(data_curvature(ids, cols, dens, rows, factors, zb, tiles))
    sums[...] = jnp.broadcast_to(lanes(known + [share]), sums.shape)


def own_components(slab, turned):
    count = turned.shape[0] // lax.axis_size("col")
    turned[...] = slab.T
    return turned[pl.ds(pl.multiple_of(lax.axis_index("col") * count, count), count), :]


def finish_kernel(sums, scalars, pieces, out):
    totals = jnp.sum(sums[...], axis=0, keepdims=True)
    n11, n12, n22, c00, c01, c10, c11, c02, c12, c22 = (totals[:, i : i + 1] for i in range(10))
    step0, turn0, a, b = trial(scalars)
    step1 = n11 / (c11 + EPS)
    h = step1 / a
    rest = 1.0 - h
    norm2 = rest * rest * n11 + 2.0 * h * rest * n12 + h * h * n22
    turn1 = norm2 / (n11 + EPS)
    g0 = -rest * turn0
    g1 = rest + turn1 - h * b
    curvature = (
        g0 * g0 * c00 + g1 * g1 * c11 + h * h * c22
        + g0 * g1 * (c01 + c10) + 2.0 * (g0 * h * c02 + g1 * h * c12)
    )
    step2 = norm2 / (curvature + EPS)
    k0, k1, k2 = step0 + step2 * g0, step1 + step2 * g1, step2 * h
    out[...] = pieces[0] + k0 * pieces[1] + k1 * pieces[2] + k2 * pieces[3]


def gather_factors(col_factors, beside):
    nrow = lax.axis_size("row")
    blocks, height, width = col_factors.shape

    def from_z(x, shift):
        return lax.ppermute(x, "row", [(i, (i - 2 * shift) % nrow) for i in range(nrow)])

    own = col_factors.reshape(1, blocks * height, width)
    near = jnp.concatenate([from_z(own, 2), own, from_z(own, 6)])
    onward = jnp.where(lax.axis_index("row") % 2 == 0, near[:1], near[2:])
    onward, near = lax.optimization_barrier((onward, near))
    onward = lax.ppermute(onward, "row", [(i, (i + (4 if i % 2 else -4)) % nrow) for i in range(nrow)])
    mine = jnp.concatenate([onward, near, from_z(near[:2], 1), from_z(near[1:], 7)])
    shifts = (4, 2, 0, 6, 3, 1, 7, 5)
    mine, beside = lax.optimization_barrier((mine, beside))
    other = lax.ppermute(mine, "row", [(i, i ^ 1) for i in range(nrow)])
    whole = jax.ShapeDtypeStruct((blocks, nrow * height, width), BF16)
    assemble = call(functools.partial(assemble_kernel, shifts), whole, [VMEM, VMEM])
    return assemble(mine, other), beside


def local(tile_values, tile_rows, tile_cols, tile_counts, col_factors, prev_factors):
    tiles = tile_values[0, 0]
    count, size = tiles.shape[0], tiles.shape[1]
    width = col_factors.shape[2]
    height_all = prev_factors.shape[0]
    blocks = height_all // size
    ncol, nrow = lax.axis_size("col"), lax.axis_size("row")
    height = height_all // ncol

    slots = count + blocks
    order = call(
        plan_kernel,
        [
            jax.ShapeDtypeStruct((slots,), jnp.int32),
            jax.ShapeDtypeStruct((slots,), jnp.int32),
            jax.ShapeDtypeStruct((slots,), F32),
            jax.ShapeDtypeStruct((slots // 2,), jnp.int32),
        ],
        [pl.ANY],
        [SMEM((3 * count,), jnp.int32), SMEM((blocks,), jnp.int32), pltpu.SemaphoreType.DMA],
        flops=BUSY,
        out_space=SMEM,
    )(jnp.concatenate([tile_rows[0, 0], tile_cols[0, 0], tile_counts[0, 0]]))
    factors, order = gather_factors(col_factors, order)
    flat = factors.reshape(-1, width)
    gram = lax.dot_general(flat, flat, (((0,), (0,)), ((), ())), preferred_element_type=F32)

    def exchange(x):
        return lax.all_to_all(x, "col", 0, 0)

    slab = jax.ShapeDtypeStruct((height_all, width), F32)
    part = jax.ShapeDtypeStruct((blocks, size, width), F32)
    wide = jax.ShapeDtypeStruct((ncol, height, width), F32)
    zb = VMEM((blocks, size, width), BF16)
    common = (*order, tiles, factors, gram)
    spaces = [SMEM] * 4 + [VMEM] * 3

    def summed(sign, partial, p):
        parts = exchange(partial.reshape(ncol, height, width))
        shard = call(functools.partial(shard_kernel, sign), wide, [VMEM, VMEM], flops=BUSY)
        return exchange(shard(parts, p))

    partial = call(apply_first, part, spaces + [VMEM])(
        *common, prev_factors.reshape(blocks, size, width)
    )
    res0 = summed(-1.0, partial, prev_factors)
    partial, q0 = call(product0_kernel, [part, slab], spaces + [VMEM], [zb])(*common, res0)
    image0 = summed(1.0, partial, q0)
    sums, own0 = call(
        dots_kernel,
        [jax.ShapeDtypeStruct((nrow, width), F32), jax.ShapeDtypeStruct((height, width), F32)],
        [VMEM] * 2,
        flops=BUSY,
    )(image0, q0)
    sums = lax.all_to_all(sums, "row", 0, 0, tiled=True)
    small = jax.ShapeDtypeStruct((8, width), F32)
    partial, q1, scalars = call(
        product1_kernel, [part, slab, small], spaces + [VMEM] * 3, [zb]
    )(*common, image0, sums, q0)
    image1 = summed(1.0, partial, q1)
    piece = (width // ncol, height_all)
    sums, pieces = call(
        product2_kernel,
        [jax.ShapeDtypeStruct((nrow * ncol, width), F32), jax.ShapeDtypeStruct((4, *piece), F32)],
        spaces + [VMEM] * 6,
        [VMEM((height_all, width), F32), zb, VMEM((4, width, height_all), F32)],
    )(*common, image1, scalars, own0, q0, q1, prev_factors)
    sums = lax.all_to_all(sums, ("row", "col"), 0, 0, tiled=True)
    return call(finish_kernel, jax.ShapeDtypeStruct(piece, F32), [VMEM] * 3)(sums, scalars, pieces)


def solution(mesh):
    return jax.shard_map(
        local,
        mesh=mesh,
        in_specs=(
            P("row", "col", None, None, None),
            P("row", "col", None),
            P("row", "col", None),
            P("row", "col", None),
            P("col", "row", None),
            P("row", None),
        ),
        out_specs=P("col", "row"),
        check_vma=False,
    )
```
